32 devices in a mesh: bx: 8 (over z, y), by: 4 (over x, core).
Axes of the slice: x: 2, y: 2, z: 4, core: 2. Of those that a mesh axis runs over, the one named last changes fastest.
Arguments:
- source: bfloat16 [8, 4, 2, 128, 1024], P('bx', 'by'), may hold values from -6 to 6
- start_tick: int32 [8, 4], P('bx', 'by'), may hold values from 0 to 3, as said below
- op_x: bfloat16 [8, 4, 2, 1024, 1024], P('bx', 'by'), may hold values from -0.09375 to 0.09375
- op_y: bfloat16 [8, 4, 2, 1024, 1024], P('bx', 'by'), may hold values from -0.09375 to 0.09375
Outputs:
- upgoing: float32 [4, 128, 2, 8, 1024], P('by', 'bx')
The draws below stay inside these ranges and needn't reach their ends.
Inputs may be any that keep to these rules, and one draw needn't show every extreme that they name: `start_tick`: both 0 and 3 occur in every draw.
All inputs are finite; a program needn't handle non-finite values.
Results may differ from the reference program's by a relative error of at most 0.012.
Values may be sent and summed in bfloat16 or wider, within the bound.
A program may use at most 64 MiB of HBM per device.

```python
import math
import jax
import jax.numpy as jnp
from jax import lax

F = 1024
SHOTS = 128
TICKS = 4
GRID_X = 8
GRID_Y = 4


def draw_start_tick(key, part):
    values = jax.random.randint(key, (GRID_X, GRID_Y), 0, TICKS)
    values = values.at[0, 0].set(0).at[GRID_X - 1, GRID_Y - 1].set(TICKS - 1)
    return values.astype(jnp.int32)


def level_of(own_key, shape, shards, smallest, top_value):
    gain = 1.0
    for dim, blocks in shards:
        draws = jax.random.uniform(jax.random.fold_in(jax.random.fold_in(own_key, 6), dim), (blocks,), jnp.float32, smallest / len(shards), top_value / len(shards))
        gain = gain * jnp.repeat(jnp.exp(draws), shape[dim] // blocks).reshape((-1,) + (1,) * (len(shape) - 1 - dim))
    return gain


def bell_draw(rng, dims, spread, limit, shards=(), kind=jnp.bfloat16):
    values = jax.random.normal(rng, dims, jnp.float32) * spread
    if len(shards) > 0:
        values = level_of(rng, dims, shards, -0.22, 0.18) * values
    return jnp.clip(values, min=-limit, max=limit).astype(kind)


def setup_inputs(seed: int = 0) -> dict:
    streams_of = jax.random.split(jax.random.key(seed), 5)
    source = bell_draw(streams_of[0], (GRID_X, GRID_Y, 2, SHOTS, F), 1.0, 6.0, ((0, 8), (1, 4)))
    start_tick = draw_start_tick(jax.random.fold_in(streams_of[4], 71), 0)
    op_x = bell_draw(streams_of[2], (GRID_X, GRID_Y, 2, F, F), (4 * F) ** -0.5, 0.09375, ((0, 8), (1, 4)))
    op_y = bell_draw(streams_of[3], (GRID_X, GRID_Y, 2, F, F), (4 * F) ** -0.5, 0.09375, ((0, 8), (1, 4)))
    return {"source": source, "start_tick": start_tick, "op_x": op_x, "op_y": op_y}


def dft_tables(length):
    indices = jnp.arange(length, dtype=jnp.int32)
    products = indices[:, None] * indices[None, :] % length
    angles = products.astype(jnp.float32) * (2.0 * math.pi / length)
    return (jnp.cos(angles).astype(jnp.bfloat16), jnp.sin(angles).astype(jnp.bfloat16))

def complex_apply(traces, operator):

    def one_row(pair):
        trace_row = pair[0].astype(jnp.float32)
        operator_row = pair[1].astype(jnp.float32)
        with_real = jnp.einsum('jcsf,jfk->jcsk', trace_row, operator_row[:, 0])
        with_imag = jnp.einsum('jcsf,jfk->jcsk', trace_row, operator_row[:, 1])
        real_out = with_real[:, 0] - with_imag[:, 1]
        imag_out = with_imag[:, 0] + with_real[:, 1]
        return jnp.stack([real_out, imag_out], axis=1)
    return lax.map(one_row, (traces, operator))

def shift_down(values, axis):
    widths = [(0, 0)] * values.ndim
    widths[axis] = (1, 0)
    kept = lax.slice_in_dim(values, 0, values.shape[axis] - 1, axis=axis)
    return jnp.pad(kept, widths)

def shift_up(values, axis):
    widths = [(0, 0)] * values.ndim
    widths[axis] = (0, 1)
    kept = lax.slice_in_dim(values, 1, values.shape[axis], axis=axis)
    return jnp.pad(kept, widths)

def reference(source, start_tick, op_x, op_y):
    east_out = jnp.zeros(source.shape, jnp.bfloat16)
    north_out = jnp.zeros(source.shape, jnp.bfloat16)
    source32 = source.astype(jnp.float32)
    for tick in range(TICKS):
        from_west = shift_down(east_out, 0).astype(jnp.float32)
        from_south = shift_down(north_out, 1).astype(jnp.float32)
        active = (start_tick <= tick).astype(jnp.float32)[:, :, None, None, None]
        incident = (from_west + from_south + active * source32).astype(jnp.bfloat16)
        east_out = complex_apply(incident, op_x).astype(jnp.bfloat16)
        north_out = complex_apply(incident, op_y).astype(jnp.bfloat16)
    mismatch = (shift_down(east_out, 0).astype(jnp.float32) + shift_down(north_out, 1).astype(jnp.float32) - shift_up(east_out, 0).astype(jnp.float32) - shift_up(north_out, 1).astype(jnp.float32)).astype(jnp.bfloat16)
    reflected = complex_apply(mismatch, op_x).astype(jnp.bfloat16)
    cos_line, sin_line = dft_tables(F)
    refl32 = reflected.astype(jnp.float32)
    cos32 = cos_line.astype(jnp.float32)
    sin32 = sin_line.astype(jnp.float32)
    spec_real = jnp.einsum('ijsf,fk->ijsk', refl32[:, :, 0], cos32) + jnp.einsum('ijsf,fk->ijsk', refl32[:, :, 1], sin32)
    spec_imag = jnp.einsum('ijsf,fk->ijsk', refl32[:, :, 1], cos32) - jnp.einsum('ijsf,fk->ijsk', refl32[:, :, 0], sin32)
    spectrum_real = spec_real.astype(jnp.bfloat16).astype(jnp.float32)
    spectrum_imag = spec_imag.astype(jnp.bfloat16).astype(jnp.float32)
    cos_grid, sin_grid = dft_tables(GRID_X)
    cosg = cos_grid.astype(jnp.float32)
    sing = sin_grid.astype(jnp.float32)
    out_real = jnp.einsum('ijsk,iq->jsqk', spectrum_real, cosg) + jnp.einsum('ijsk,iq->jsqk', spectrum_imag, sing)
    out_imag = jnp.einsum('ijsk,iq->jsqk', spectrum_imag, cosg) - jnp.einsum('ijsk,iq->jsqk', spectrum_real, sing)
    wave_index = jnp.arange(GRID_X, dtype=jnp.int32)
    signed = jnp.where(wave_index < GRID_X // 2, wave_index, wave_index - GRID_X).astype(jnp.float32)
    weights = 0.5 * (1.0 + signed / jnp.sqrt(signed * signed + 1.0))
    return jnp.stack([out_real, out_imag], axis=2) * weights[None, None, None, :, None]
```

```python
import functools
import math

import jax
import jax.numpy as jnp
import ml_dtypes
import numpy as np
from jax import lax
from jax.experimental import pallas as pl
from jax.experimental.pallas import tpu as pltpu
from jax.sharding import PartitionSpec as P

TICKS = 4
CHUNKS = 4
MESH = pl.DeviceIdType.MESH
BF16 = jnp.bfloat16
F32 = jnp.float32


def dft_tables(length):
    indices = np.arange(length, dtype=np.int64)
    angles = (indices[:, None] * indices[None, :] % length) * (2.0 * math.pi / length)
    return np.cos(angles).astype(ml_dtypes.bfloat16), np.sin(angles).astype(ml_dtypes.bfloat16)


def grid_gain(pieces):
    wave = np.arange(pieces)
    signed = np.where(wave < pieces // 2, wave, wave - pieces).astype(np.float64)
    return (0.5 * (1.0 + signed / np.sqrt(signed * signed + 1.0))).astype(np.float32)


def grid_matrix(pieces, owned):
    cos_grid, sin_grid = (t.astype(np.float32) for t in dft_tables(pieces))
    parts = np.zeros((2, pieces, pieces, 2), np.float32)
    parts[0, :, :, 0] = cos_grid.T
    parts[0, :, :, 1] = sin_grid.T
    parts[1, :, :, 0] = -sin_grid.T
    parts[1, :, :, 1] = cos_grid.T
    full = np.einsum("cqir,st->scqirt", parts, np.eye(owned, dtype=np.float32))
    side = 2 * pieces * owned
    return full.reshape(side, side).astype(ml_dtypes.bfloat16)


def kernel(
    plan,
    first_ref, source_ref, opx_hbm, opy_hbm, line_hbm, grid_ref, gain_ref,
    out_ref,
    opx, opy, line, left, e_out, n_out, e_in, n_in, relay_in, d_out, d_in, nf_in, nb_in, spec, regroup,
    load_sem, e_send, e_recv, n_send, n_recv, r_send, r_recv, d_send, d_recv,
    nf_send, nf_recv, nb_send, nb_recv, s_send, s_recv,
):
    pieces, rows_by, per, group, fused = plan
    chunks = CHUNKS
    half = per * group
    width = source_ref.shape[2]
    tile = min(256, width)
    i, j = lax.axis_index("bx"), lax.axis_index("by")
    odd = lax.rem(i, 2)
    partner = i + 1 - 2 * odd
    relay_to = i - 2 + 4 * odd
    relay_from = i + 2 - 4 * odd
    has_relay_to = (relay_to >= 0) & (relay_to < pieces)
    has_relay_from = (relay_from >= 0) & (relay_from < pieces)

    loads = [
        pltpu.make_async_copy(src, dst, load_sem.at[k])
        for k, (src, dst) in enumerate(((opx_hbm, opx), (opy_hbm, opy), (line_hbm, line)))
    ]
    for load in loads:
        load.start()

    barrier = pltpu.get_barrier_semaphore()
    for k in range(1, pieces):
        pl.semaphore_signal(
            barrier, inc=1, device_id={"bx": lax.rem(i + k, pieces)}, device_id_type=MESH
        )

    @pl.when(j > 0)
    def _():
        pl.semaphore_signal(barrier, inc=1, device_id={"by": j - 1}, device_id_type=MESH)

    @pl.when(j < rows_by - 1)
    def _():
        pl.semaphore_signal(barrier, inc=1, device_id={"by": j + 1}, device_id_type=MESH)

    def clear(ref, tick, c):
        ref[tick, c] = jnp.zeros(ref.shape[2:], ref.dtype)

    def clear_all(c, _):
        clear(e_in, 0, c)
        clear(n_in, 0, c)

        @pl.when(i == 0)
        def _():
            for tick in range(1, TICKS):
                clear(e_in, tick, c)

        @pl.when(j == 0)
        def _():
            for tick in range(1, TICKS):
                clear(n_in, tick, c)
            nf_in[c] = jnp.zeros(nf_in.shape[1:], BF16)

        @pl.when(j == rows_by - 1)
        def _():
            nb_in[c] = jnp.zeros(nb_in.shape[1:], BF16)

        @pl.when(jnp.logical_not(has_relay_from))
        def _():
            relay_in[c] = jnp.zeros(relay_in.shape[1:], BF16)

        return 0

    lax.fori_loop(0, chunks, clear_all, 0)

    peers = pieces - 1 + (j > 0).astype(jnp.int32) + (j < rows_by - 1).astype(jnp.int32)
    pl.semaphore_wait(barrier, peers)

    def remote(src, dst, send, recv, where):
        return pltpu.make_async_remote_copy(
            src_ref=src, dst_ref=dst, send_sem=send, recv_sem=recv, device_id=where, device_id_type=MESH
        )

    def east(tick, c):
        return remote(
            e_out.at[tick, c], e_in.at[tick + 1, c], e_send.at[tick, c], e_recv.at[tick, c], {"bx": i + 1}
        )

    def north(tick, c):
        return remote(
            n_out.at[tick, c], n_in.at[tick + 1, c], n_send.at[tick, c], n_recv.at[tick, c], {"by": j + 1}
        )

    def relay(c):
        return remote(
            e_out.at[TICKS - 1, c], relay_in.at[c], r_send.at[c], r_recv.at[c], {"bx": relay_to}
        )

    def difference(c):
        return remote(d_out.at[c], d_in.at[c], d_send.at[c], d_recv.at[c], {"bx": partner})

    def final_north(c):
        return remote(n_out.at[TICKS - 1, c], nf_in.at[c], nf_send.at[c], nf_recv.at[c], {"by": j + 1})

    def final_south(c):
        return remote(n_out.at[TICKS - 1, c], nb_in.at[c], nb_send.at[c], nb_recv.at[c], {"by": j - 1})

    def owner(c, o):
        if o % 2 == 1 and chunks % 2 == 0:
            return c + 1 - 2 * lax.rem(c, 2) + chunks * o
        return c + chunks * o

    def regrouped(c, o):
        return remote(
            spec.at[c, o], regroup.at[i], s_send.at[c, o], s_recv.at[i], {"bx": owner(c, o)}
        )

    def shot_rows(c, o):
        return pl.ds(pl.multiple_of(owner(c, o) * group, group), group)

    def place(part, at, size, value):
        if part == 0:
            left[at : at + size, :width] = value
            left[half + at : half + at + size, width:] = value
        else:
            left[at : at + size, width:] = -value
            left[half + at : half + at + size, :width] = value

    def product(matrix, put):
        for start in range(0, width, tile):
            cols = slice(start, start + tile)
            got = jnp.dot(left[...], matrix[:, cols], preferred_element_type=F32)
            put(cols, got.astype(BF16))

    def incident(tick, c):
        active = (first_ref[0, 0] <= tick).astype(F32)
        for part in range(2):
            for o in range(per):
                at = o * group
                rows = slice(part * half + at, part * half + at + group)
                value = (
                    e_in[tick, c, rows, :].astype(F32)
                    + n_in[tick, c, rows, :].astype(F32)
                    + active * source_ref[part, shot_rows(c, o), :].astype(F32)
                )
                place(part, at, group, value.astype(BF16))

    def arrive(tick, c):
        @pl.when(i > 0)
        def _():
            east(tick - 1, c).wait_recv()

        @pl.when(j > 0)
        def _():
            north(tick - 1, c).wait_recv()

    def sweep(step, _):
        tick, c = step // chunks, lax.rem(step, chunks)

        @pl.when(tick > 0)
        def _():
            arrive(tick, c)

        incident(tick, c)

        @pl.when(step == 0)
        def _():
            loads[0].wait()

        def put_east(cols, value):
            e_out[tick, c, :, cols] = value

        product(opx, put_east)

        @pl.when(i < pieces - 1)
        def _():
            east(tick, c).start()

        @pl.when(step == 0)
        def _():
            loads[1].wait()

        def put_north(cols, value):
            n_out[tick, c, :, cols] = value

        product(opy, put_north)

        @pl.when(j < rows_by - 1)
        def _():
            north(tick, c).start()

        return 0

    lax.fori_loop(0, (TICKS - 1) * chunks, sweep, 0)
    loads[2].wait()
    last = TICKS - 1

    def last_tick(c):
        arrive(last, c)
        incident(last, c)

        def put_east(cols, value):
            e_out[last, c, :, cols] = value

        product(opx, put_east)

        @pl.when(has_relay_to)
        def _():
            relay(c).start()

        def put_north(cols, value):
            n_out[last, c, :, cols] = value

        product(opy, put_north)

        @pl.when(j < rows_by - 1)
        def _():
            final_north(c).start()

        @pl.when(j > 0)
        def _():
            final_south(c).start()

    def subtract(c):
        @pl.when(has_relay_from)
        def _():
            relay(c).wait_recv()

        sign = (2 * odd - 1).astype(F32)
        d_out[c] = (sign * (relay_in[c].astype(F32) - e_out[last, c].astype(F32))).astype(BF16)
        difference(c).start()

    def reflect(c):
        difference(c).wait_recv()

        @pl.when(j > 0)
        def _():
            final_north(c).wait_recv()

        @pl.when(j < rows_by - 1)
        def _():
            final_south(c).wait_recv()

        for part in range(2):
            rows = slice(part * half, (part + 1) * half)
            value = (
                d_in[c, rows, :].astype(F32) + nf_in[c, rows, :].astype(F32) - nb_in[c, rows, :].astype(F32)
            )
            place(part, 0, half, value.astype(BF16))

        def put_reflected(cols, value):
            d_out_free[:, cols] = value

        d_out_free = e_in.at[0, c]
        product(opx, put_reflected)
        for part in range(2):
            place(part, 0, half, d_out_free[part * half : (part + 1) * half, :])

        def put_spectrum(cols, value):
            for part in range(2):
                for o in range(per):
                    at = part * half + o * group
                    if fused:
                        spec[c, o, part * group : (part + 1) * group, cols] = value[at : at + group]
                    else:
                        out_ref[part, shot_rows(c, o), cols] = value[at : at + group]

        product(line, put_spectrum)
        if fused:
            for o in range(per):
                @pl.when(owner(c, o) == i)
                def _():
                    regroup[i] = spec[c, o]

                @pl.when(owner(c, o) != i)
                def _():
                    regrouped(c, o).start()

    def finish(step, _):
        @pl.when(step < chunks)
        def _():
            last_tick(step)

        @pl.when((step >= 1) & (step <= chunks))
        def _():
            subtract(step - 1)

        @pl.when(step >= 2)
        def _():
            reflect(step - 2)

        return 0

    lax.fori_loop(0, chunks + 2, finish, 0)

    def sent(c, _):
        for tick in range(TICKS - 1):
            @pl.when(i < pieces - 1)
            def _():
                east(tick, c).wait_send()

            @pl.when(j < rows_by - 1)
            def _():
                north(tick, c).wait_send()

        @pl.when(has_relay_to)
        def _():
            relay(c).wait_send()

        @pl.when(j < rows_by - 1)
        def _():
            final_north(c).wait_send()

        @pl.when(j > 0)
        def _():
            final_south(c).wait_send()

        difference(c).wait_send()
        return 0

    lax.fori_loop(0, chunks, sent, 0)

    if fused:
        for k in range(1, pieces):
            peer = lax.rem(i + k, pieces)
            remote(
                spec.at[0, 0], regroup.at[peer], s_send.at[0, 0], s_recv.at[peer], {"bx": peer}
            ).wait_recv()
        whole = regroup[...].reshape(2 * pieces * group, width)
        for start in range(0, width, tile):
            cols = slice(start, start + tile)
            got = jnp.dot(grid_ref[...], whole[:, cols], preferred_element_type=F32)
            out_ref[:, cols] = got * gain_ref[:, :1]
        for c in range(chunks):
            for o in range(per):
                @pl.when(owner(c, o) != i)
                def _():
                    regrouped(c, o).wait_send()


def shards(source, start_tick, op_x, op_y):
    pieces, rows_by = lax.axis_size("bx"), lax.axis_size("by")
    _, _, _, shots, width = source.shape
    owned = shots // pieces
    fused = owned % 16 == 0 and pieces % CHUNKS == 0
    per, group = (pieces // CHUNKS, owned) if fused else (1, shots // CHUNKS)
    rows = 2 * per * group
    side = 2 * pieces * owned

    cos_line, sin_line = dft_tables(width)
    line = jnp.asarray(np.concatenate([cos_line, -sin_line]))
    grid = jnp.asarray(grid_matrix(pieces, owned))
    gain = jnp.asarray(np.repeat(np.tile(grid_gain(pieces), 2 * owned)[:, None], 128, axis=1))

    vmem = pl.BlockSpec(memory_space=pltpu.VMEM)
    anywhere = pl.BlockSpec(memory_space=pl.ANY)
    out_shape = (
        jax.ShapeDtypeStruct((side, width), F32) if fused else jax.ShapeDtypeStruct((2, shots, width), BF16)
    )
    ticked = pltpu.VMEM((TICKS, CHUNKS, rows, width), BF16)
    single = pltpu.VMEM((CHUNKS, rows, width), BF16)
    operator = pltpu.VMEM((2 * width, width), BF16)
    ticked_sem = pltpu.SemaphoreType.DMA((TICKS - 1, CHUNKS))
    single_sem = pltpu.SemaphoreType.DMA((CHUNKS,))
    result = pl.pallas_call(
        functools.partial(kernel, (pieces, rows_by, per, group, fused)),
        out_shape=out_shape,
        in_specs=[pl.BlockSpec(memory_space=pltpu.SMEM), vmem, anywhere, anywhere, anywhere, vmem, vmem],
        out_specs=vmem,
        scratch_shapes=[
            operator, operator, operator,
            pltpu.VMEM((rows, 2 * width), BF16),
            ticked, ticked, ticked, ticked,
            single, single, single, single, single,
            pltpu.VMEM((CHUNKS, per, 2 * group, width), BF16),
            pltpu.VMEM((pieces, 2 * group, width) if fused else (1, 16, 128), BF16),
            pltpu.SemaphoreType.DMA((3,)),
            ticked_sem, ticked_sem, ticked_sem, ticked_sem,
            single_sem, single_sem, single_sem, single_sem,
            single_sem, single_sem, single_sem, single_sem,
            pltpu.SemaphoreType.DMA((CHUNKS, per)),
            pltpu.SemaphoreType.DMA((pieces,)),
        ],
        compiler_params=pltpu.CompilerParams(
            collective_id=0, has_side_effects=True, vmem_limit_bytes=48 * 1024 * 1024
        ),
        cost_estimate=pl.CostEstimate(
            flops=2 * rows * CHUNKS * 2 * width * width * 10, bytes_accessed=16 * width * width, transcendentals=0
        ),
    )(
        start_tick,
        source[0, 0],
        op_x.reshape(2 * width, width),
        op_y.reshape(2 * width, width),
        line,
        grid,
        gain,
    )
    if fused:
        return result.reshape(1, owned, 2, pieces, width)
    arranged = result.reshape(2, pieces, owned, 1, width)
    spectrum = lax.all_to_all(arranged, "bx", split_axis=1, concat_axis=3, tiled=True)
    received = spectrum.reshape(2, owned, pieces, width)
    cos_grid, sin_grid = (jnp.asarray(t) for t in dft_tables(pieces))

    def over_grid(values, table):
        return jnp.einsum("sik,iq->sqk", values, table, preferred_element_type=F32)

    out_real = over_grid(received[0], cos_grid) + over_grid(received[1], sin_grid)
    out_imag = over_grid(received[1], cos_grid) - over_grid(received[0], sin_grid)
    upgoing = jnp.stack([out_real, out_imag], axis=1) * grid_gain(pieces)[None, None, :, None]
    return upgoing[None]


def solution(mesh):
    placed = (
        P("bx", "by", None, None, None),
        P("bx", "by"),
        P("bx", "by", None, None, None),
        P("bx", "by", None, None, None),
    )
    return jax.shard_map(
        shards,
        mesh=mesh,
        in_specs=placed,
        out_specs=P("by", "bx", None, None, None),
        check_vma=False,
    )
```

```python
import functools
import math

import jax
import jax.numpy as jnp
import ml_dtypes
import numpy as np
from jax import lax
from jax.experimental import pallas as pl
from jax.experimental.pallas import tpu as pltpu
from jax.sharding import PartitionSpec as P

TICKS = 4
CHUNKS = 4
MESH = pl.DeviceIdType.MESH
BF16 = jnp.bfloat16
F32 = jnp.float32


def dft_tables(length):
    indices = np.arange(length, dtype=np.int64)
    angles = (indices[:, None] * indices[None, :] % length) * (2.0 * math.pi / length)
    return np.cos(angles).astype(ml_dtypes.bfloat16), np.sin(angles).astype(ml_dtypes.bfloat16)


def grid_gain(pieces):
    wave = np.arange(pieces)
    signed = np.where(wave < pieces // 2, wave, wave - pieces).astype(np.float64)
    return (0.5 * (1.0 + signed / np.sqrt(signed * signed + 1.0))).astype(np.float32)


def grid_matrix(pieces, owned):
    cos_grid, sin_grid = (t.astype(np.float32) for t in dft_tables(pieces))
    parts = np.zeros((2, pieces, pieces, 2), np.float32)
    parts[0, :, :, 0] = cos_grid.T
    parts[0, :, :, 1] = sin_grid.T
    parts[1, :, :, 0] = -sin_grid.T
    parts[1, :, :, 1] = cos_grid.T
    full = np.einsum("cqir,st->scqirt", parts, np.eye(owned, dtype=np.float32))
    side = 2 * pieces * owned
    return full.reshape(side, side).astype(ml_dtypes.bfloat16)


def kernel(
    plan,
    first_ref, source_hbm, opx_hbm, opy_hbm, line_hbm, grid_hbm, gain_hbm,
    out_ref,
    source_ref, opx, opy, line, grid_ref, gain_ref, left, e_out, n_out, e_in, n_in, relay_in, d_out, d_in, nf_in, nb_in, spec, regroup,
    load_sem, e_send, e_recv, n_send, n_recv, r_send, r_recv, d_send, d_recv,
    nf_send, nf_recv, nb_send, nb_recv, s_send, s_recv,
):
    pieces, rows_by, per, group, fused = plan
    chunks = CHUNKS
    half = per * group
    width = source_hbm.shape[2]
    tile = min(256, width)
    i, j = lax.axis_index("bx"), lax.axis_index("by")
    odd = lax.rem(i, 2)
    partner = i + 1 - 2 * odd
    relay_to = i - 2 + 4 * odd
    relay_from = i + 2 - 4 * odd
    has_relay_to = (relay_to >= 0) & (relay_to < pieces)
    has_relay_from = (relay_from >= 0) & (relay_from < pieces)

    starts = range(0, width, tile)

    def load(src, dst, k):
        return pltpu.make_async_copy(src, dst, load_sem.at[k])

    def by_tiles(src, dst, k):
        return [
            load(src.at[:, start : start + tile], dst.at[:, start : start + tile], k + n)
            for n, start in enumerate(starts)
        ]

    count = len(starts)
    source_load = load(source_hbm, source_ref, 0)
    opx_loads = by_tiles(opx_hbm, opx, 1)
    opy_loads = by_tiles(opy_hbm, opy, 1 + count)
    late_loads = [
        load(line_hbm, line, 1 + 2 * count),
        load(grid_hbm, grid_ref, 2 + 2 * count),
        load(gain_hbm, gain_ref, 3 + 2 * count),
    ]
    for copy in [source_load, *opx_loads, *opy_loads]:
        copy.start()

    barrier = pltpu.get_barrier_semaphore()
    for k in range(1, pieces):
        pl.semaphore_signal(
            barrier, inc=1, device_id={"bx": lax.rem(i + k, pieces)}, device_id_type=MESH
        )

    @pl.when(j > 0)
    def _():
        pl.semaphore_signal(barrier, inc=1, device_id={"by": j - 1}, device_id_type=MESH)

    @pl.when(j < rows_by - 1)
    def _():
        pl.semaphore_signal(barrier, inc=1, device_id={"by": j + 1}, device_id_type=MESH)

    def clear(ref, tick, c):
        ref[tick, c] = jnp.zeros(ref.shape[2:], ref.dtype)

    def clear_all(c, _):
        clear(e_in, 0, c)
        clear(n_in, 0, c)

        @pl.when(i == 0)
        def _():
            for tick in range(1, TICKS):
                clear(e_in, tick, c)

        @pl.when(j == 0)
        def _():
            for tick in range(1, TICKS):
                clear(n_in, tick, c)
            nf_in[c] = jnp.zeros(nf_in.shape[1:], BF16)

        @pl.when(j == rows_by - 1)
        def _():
            nb_in[c] = jnp.zeros(nb_in.shape[1:], BF16)

        @pl.when(jnp.logical_not(has_relay_from))
        def _():
            relay_in[c] = jnp.zeros(relay_in.shape[1:], BF16)

        return 0

    lax.fori_loop(0, chunks, clear_all, 0)

    peers = pieces - 1 + (j > 0).astype(jnp.int32) + (j < rows_by - 1).astype(jnp.int32)
    pl.semaphore_wait(barrier, peers)

    def remote(src, dst, send, recv, where):
        return pltpu.make_async_remote_copy(
            src_ref=src, dst_ref=dst, send_sem=send, recv_sem=recv, device_id=where, device_id_type=MESH
        )

    def east(tick, c):
        return remote(
            e_out.at[tick, c], e_in.at[tick + 1, c], e_send.at[tick, c], e_recv.at[tick, c], {"bx": i + 1}
        )

    def north(tick, c):
        return remote(
            n_out.at[tick, c], n_in.at[tick + 1, c], n_send.at[tick, c], n_recv.at[tick, c], {"by": j + 1}
        )

    def relay(c):
        return remote(
            e_out.at[TICKS - 1, c], relay_in.at[c], r_send.at[c], r_recv.at[c], {"bx": relay_to}
        )

    def difference(c):
        return remote(d_out.at[c], d_in.at[c], d_send.at[c], d_recv.at[c], {"bx": partner})

    def final_north(c):
        return remote(n_out.at[TICKS - 1, c], nf_in.at[c], nf_send.at[c], nf_recv.at[c], {"by": j + 1})

    def final_south(c):
        return remote(n_out.at[TICKS - 1, c], nb_in.at[c], nb_send.at[c], nb_recv.at[c], {"by": j - 1})

    def owner(c, o):
        if o % 2 == 1:
            return pieces - 1 - c - chunks * (o // 2)
        return c + chunks * (o // 2)

    def regrouped(c, o):
        return remote(
            spec.at[c, o], regroup.at[i], s_send.at[c, o], s_recv.at[i], {"bx": owner(c, o)}
        )

    def shot_rows(c, o):
        return pl.ds(pl.multiple_of(owner(c, o) * group, group), group)

    def place(part, at, size, value):
        if part == 0:
            left[at : at + size, :width] = value
            left[half + at : half + at + size, width:] = value
        else:
            left[at : at + size, width:] = -value
            left[half + at : half + at + size, :width] = value

    def product(matrix, put, loads=None, first=None):
        for n, start in enumerate(starts):
            cols = slice(start, start + tile)
            if loads is not None:
                pl.when(first)(loads[n].wait)
            got = jnp.dot(left[...], matrix[:, cols], preferred_element_type=F32)
            put(cols, got.astype(BF16))

    def incident(tick, c):
        active = (first_ref[0, 0] <= tick).astype(F32)
        for part in range(2):
            for o in range(per):
                at = o * group
                rows = slice(part * half + at, part * half + at + group)
                value = (
                    e_in[tick, c, rows, :].astype(F32)
                    + n_in[tick, c, rows, :].astype(F32)
                    + active * source_ref[part, shot_rows(c, o), :].astype(F32)
                )
                place(part, at, group, value.astype(BF16))

    def arrive(tick, c):
        @pl.when(i > 0)
        def _():
            east(tick - 1, c).wait_recv()

        @pl.when(j > 0)
        def _():
            north(tick - 1, c).wait_recv()

    def sweep(step, _):
        tick, c = step // chunks, lax.rem(step, chunks)

        @pl.when(tick > 0)
        def _():
            arrive(tick, c)

        incident(tick, c)

        def put_east(cols, value):
            e_out[tick, c, :, cols] = value

        product(opx, put_east, opx_loads, step == 0)

        @pl.when(i < pieces - 1)
        def _():
            east(tick, c).start()

        def put_north(cols, value):
            n_out[tick, c, :, cols] = value

        product(opy, put_north, opy_loads, step == 0)

        @pl.when(j < rows_by - 1)
        def _():
            north(tick, c).start()

        return 0

    source_load.wait()
    lax.fori_loop(0, chunks, sweep, 0)
    for copy in late_loads:
        copy.start()
    lax.fori_loop(chunks, (TICKS - 1) * chunks, sweep, 0)
    for copy in late_loads:
        copy.wait()
    last = TICKS - 1

    def last_tick(c):
        arrive(last, c)
        incident(last, c)

        def put_east(cols, value):
            e_out[last, c, :, cols] = value

        product(opx, put_east)

        @pl.when(has_relay_to)
        def _():
            relay(c).start()

        def put_north(cols, value):
            n_out[last, c, :, cols] = value

        product(opy, put_north)

        @pl.when(j < rows_by - 1)
        def _():
            final_north(c).start()

        @pl.when(j > 0)
        def _():
            final_south(c).start()

    def subtract(c):
        @pl.when(has_relay_from)
        def _():
            relay(c).wait_recv()

        sign = (2 * odd - 1).astype(F32)
        d_out[c] = (sign * (relay_in[c].astype(F32) - e_out[last, c].astype(F32))).astype(BF16)
        difference(c).start()

    def reflect(c):
        difference(c).wait_recv()

        @pl.when(j > 0)
        def _():
            final_north(c).wait_recv()

        @pl.when(j < rows_by - 1)
        def _():
            final_south(c).wait_recv()

        for part in range(2):
            rows = slice(part * half, (part + 1) * half)
            value = (
                d_in[c, rows, :].astype(F32) + nf_in[c, rows, :].astype(F32) - nb_in[c, rows, :].astype(F32)
            )
            place(part, 0, half, value.astype(BF16))

        def put_reflected(cols, value):
            d_out_free[:, cols] = value

        d_out_free = e_in.at[0, c]
        product(opx, put_reflected)
        for part in range(2):
            place(part, 0, half, d_out_free[part * half : (part + 1) * half, :])

        def put_spectrum(cols, value):
            for part in range(2):
                for o in range(per):
                    at = part * half + o * group
                    if fused:
                        spec[c, o, part * group : (part + 1) * group, cols] = value[at : at + group]
                    else:
                        out_ref[part, shot_rows(c, o), cols] = value[at : at + group]

        product(line, put_spectrum)
        if fused:
            for o in range(per):
                @pl.when(owner(c, o) == i)
                def _():
                    regroup[i] = spec[c, o]

                @pl.when(owner(c, o) != i)
                def _():
                    regrouped(c, o).start()

    def finish(step, _):
        @pl.when(step < chunks)
        def _():
            last_tick(step)

        @pl.when((step >= 1) & (step <= chunks))
        def _():
            subtract(step - 1)

        @pl.when(step >= 2)
        def _():
            reflect(step - 2)

        return 0

    lax.fori_loop(0, chunks + 2, finish, 0)

    def sent(c, _):
        for tick in range(TICKS - 1):
            @pl.when(i < pieces - 1)
            def _():
                east(tick, c).wait_send()

            @pl.when(j < rows_by - 1)
            def _():
                north(tick, c).wait_send()

        @pl.when(has_relay_to)
        def _():
            relay(c).wait_send()

        @pl.when(j < rows_by - 1)
        def _():
            final_north(c).wait_send()

        @pl.when(j > 0)
        def _():
            final_south(c).wait_send()

        difference(c).wait_send()
        return 0

    lax.fori_loop(0, chunks, sent, 0)

    if fused:
        for k in range(1, pieces):
            peer = lax.rem(i + k, pieces)
            remote(
                spec.at[0, 0], regroup.at[peer], s_send.at[0, 0], s_recv.at[peer], {"bx": peer}
            ).wait_recv()
        whole = regroup[...].reshape(2 * pieces * group, width)
        for start in range(0, width, tile):
            cols = slice(start, start + tile)
            got = jnp.dot(grid_ref[...], whole[:, cols], preferred_element_type=F32)
            out_ref[:, cols] = got * gain_ref[:, :1]
        for c in range(chunks):
            for o in range(per):
                @pl.when(owner(c, o) != i)
                def _():
                    regrouped(c, o).wait_send()


def shards(source, start_tick, op_x, op_y):
    pieces, rows_by = lax.axis_size("bx"), lax.axis_size("by")
    _, _, _, shots, width = source.shape
    owned = shots // pieces
    fused = owned % 16 == 0 and pieces % (2 * CHUNKS) == 0
    per, group = (pieces // CHUNKS, owned) if fused else (1, shots // CHUNKS)
    rows = 2 * per * group
    side = 2 * pieces * owned

    cos_line, sin_line = dft_tables(width)
    line = jnp.asarray(np.concatenate([cos_line, -sin_line]))
    grid = jnp.asarray(grid_matrix(pieces, owned))
    gain = jnp.asarray(np.repeat(np.tile(grid_gain(pieces), 2 * owned)[:, None], 128, axis=1))

    out_shape = (
        jax.ShapeDtypeStruct((side, width), F32) if fused else jax.ShapeDtypeStruct((2, shots, width), BF16)
    )
    ticked = pltpu.VMEM((TICKS, CHUNKS, rows, width), BF16)
    single = pltpu.VMEM((CHUNKS, rows, width), BF16)
    operator = pltpu.VMEM((2 * width, width), BF16)
    ticked_sem = pltpu.SemaphoreType.DMA((TICKS - 1, CHUNKS))
    single_sem = pltpu.SemaphoreType.DMA((CHUNKS,))
    result = pl.pallas_call(
        functools.partial(kernel, (pieces, rows_by, per, group, fused)),
        out_shape=out_shape,
        in_specs=[pl.BlockSpec(memory_space=pltpu.SMEM)] + [pl.BlockSpec(memory_space=pl.ANY)] * 6,
        out_specs=pl.BlockSpec(memory_space=pltpu.VMEM),
        scratch_shapes=[
            pltpu.VMEM((2, shots, width), BF16),
            operator, operator, operator,
            pltpu.VMEM((side, side), BF16),
            pltpu.VMEM((side, 128), F32),
            pltpu.VMEM((rows, 2 * width), BF16),
            ticked, ticked, ticked, ticked,
            single, single, single, single, single,
            pltpu.VMEM((CHUNKS, per, 2 * group, width), BF16),
            pltpu.VMEM((pieces, 2 * group, width) if fused else (1, 16, 128), BF16),
            pltpu.SemaphoreType.DMA((4 + 2 * pl.cdiv(width, 256),)),
            ticked_sem, ticked_sem, ticked_sem, ticked_sem,
            single_sem, single_sem, single_sem, single_sem,
            single_sem, single_sem, single_sem, single_sem,
            pltpu.SemaphoreType.DMA((CHUNKS, per)),
            pltpu.SemaphoreType.DMA((pieces,)),
        ],
        compiler_params=pltpu.CompilerParams(
            collective_id=0, has_side_effects=True, vmem_limit_bytes=63 * 1024 * 1024
        ),
        cost_estimate=pl.CostEstimate(
            flops=2 * rows * CHUNKS * 2 * width * width * 10, bytes_accessed=16 * width * width, transcendentals=0
        ),
    )(
        start_tick,
        source[0, 0],
        op_x.reshape(2 * width, width),
        op_y.reshape(2 * width, width),
        line,
        grid,
        gain,
    )
    if fused:
        return result.reshape(1, owned, 2, pieces, width)
    arranged = result.reshape(2, pieces, owned, 1, width)
    spectrum = lax.all_to_all(arranged, "bx", split_axis=1, concat_axis=3, tiled=True)
    received = spectrum.reshape(2, owned, pieces, width)
    cos_grid, sin_grid = (jnp.asarray(t) for t in dft_tables(pieces))

    def over_grid(values, table):
        return jnp.einsum("sik,iq->sqk", values, table, preferred_element_type=F32)

    out_real = over_grid(received[0], cos_grid) + over_grid(received[1], sin_grid)
    out_imag = over_grid(received[1], cos_grid) - over_grid(received[0], sin_grid)
    upgoing = jnp.stack([out_real, out_imag], axis=1) * grid_gain(pieces)[None, None, :, None]
    return upgoing[None]


def solution(mesh):
    placed = (
        P("bx", "by", None, None, None),
        P("bx", "by"),
        P("bx", "by", None, None, None),
        P("bx", "by", None, None, None),
    )
    return jax.shard_map(
        shards,
        mesh=mesh,
        in_specs=placed,
        out_specs=P("by", "bx", None, None, None),
        check_vma=False,
    )
```

```python
import functools
import math

import jax
import jax.numpy as jnp
import ml_dtypes
import numpy as np
from jax import lax
from jax.experimental import pallas as pl
from jax.experimental.pallas import tpu as pltpu
from jax.sharding import PartitionSpec as P

TICKS = 4
CHUNKS = 2
MESH = pl.DeviceIdType.MESH
BF16 = jnp.bfloat16
F32 = jnp.float32


def dft_tables(length):
    indices = np.arange(length, dtype=np.int64)
    angles = (indices[:, None] * indices[None, :] % length) * (2.0 * math.pi / length)
    return np.cos(angles).astype(ml_dtypes.bfloat16), np.sin(angles).astype(ml_dtypes.bfloat16)


def grid_gain(pieces):
    wave = np.arange(pieces)
    signed = np.where(wave < pieces // 2, wave, wave - pieces).astype(np.float64)
    return (0.5 * (1.0 + signed / np.sqrt(signed * signed + 1.0))).astype(np.float32)


def grid_matrix(pieces, owned):
    cos_grid, sin_grid = (t.astype(np.float32) for t in dft_tables(pieces))
    parts = np.zeros((2, pieces, pieces, 2), np.float32)
    parts[0, :, :, 0] = cos_grid.T
    parts[0, :, :, 1] = sin_grid.T
    parts[1, :, :, 0] = -sin_grid.T
    parts[1, :, :, 1] = cos_grid.T
    full = np.einsum("cqir,st->scqirt", parts, np.eye(owned, dtype=np.float32))
    side = 2 * pieces * owned
    return full.reshape(side, side).astype(ml_dtypes.bfloat16)


def kernel(
    plan,
    first_ref, source_hbm, opx_hbm, opy_hbm, tables_hbm,
    out_ref,
    source_ref, opx, opy, tables, left, e_out, n_out, e_in, n_in, relay_in, d_out, d_in, nf_in, nb_in, spec, regroup,
    load_sem, e_send, e_recv, n_send, n_recv, r_send, r_recv, d_send, d_recv,
    nf_send, nf_recv, nb_send, nb_recv, s_send, s_recv,
):
    pieces, rows_by, per, group, fused = plan
    chunks = CHUNKS
    half = per * group
    width = source_hbm.shape[2]
    tile = min(256, width)
    i, j = lax.axis_index("bx"), lax.axis_index("by")
    odd = lax.rem(i, 2)
    partner = i + 1 - 2 * odd
    relay_to = i - 2 + 4 * odd
    relay_from = i + 2 - 4 * odd
    has_relay_to = (relay_to >= 0) & (relay_to < pieces)
    has_relay_from = (relay_from >= 0) & (relay_from < pieces)

    starts = range(0, width, tile)

    def load(src, dst, k):
        return pltpu.make_async_copy(src, dst, load_sem.at[k])

    def by_tiles(src, dst, k):
        return [
            load(src.at[:, start : start + tile], dst.at[:, start : start + tile], k + n)
            for n, start in enumerate(starts)
        ]

    count = len(starts)
    source_load = load(source_hbm, source_ref, 0)
    opx_loads = by_tiles(opx_hbm, opx, 1)
    opy_loads = by_tiles(opy_hbm, opy, 1 + count)
    tables_load = load(tables_hbm, tables, 1 + 2 * count)
    for copy in [source_load, *opx_loads, *opy_loads]:
        copy.start()

    barrier = pltpu.get_barrier_semaphore()
    for k in range(1, pieces):
        pl.semaphore_signal(
            barrier, inc=1, device_id={"bx": lax.rem(i + k, pieces)}, device_id_type=MESH
        )

    @pl.when(j > 0)
    def _():
        pl.semaphore_signal(barrier, inc=1, device_id={"by": j - 1}, device_id_type=MESH)

    @pl.when(j < rows_by - 1)
    def _():
        pl.semaphore_signal(barrier, inc=1, device_id={"by": j + 1}, device_id_type=MESH)

    def clear(ref, tick, c):
        ref[tick, c] = jnp.zeros(ref.shape[2:], ref.dtype)

    def clear_all(c, _):
        clear(e_in, 0, c)
        clear(n_in, 0, c)

        @pl.when(i == 0)
        def _():
            for tick in range(1, TICKS):
                clear(e_in, tick, c)

        @pl.when(j == 0)
        def _():
            for tick in range(1, TICKS):
                clear(n_in, tick, c)
            nf_in[c] = jnp.zeros(nf_in.shape[1:], BF16)

        @pl.when(j == rows_by - 1)
        def _():
            nb_in[c] = jnp.zeros(nb_in.shape[1:], BF16)

        @pl.when(jnp.logical_not(has_relay_from))
        def _():
            relay_in[c] = jnp.zeros(relay_in.shape[1:], BF16)

        return 0

    lax.fori_loop(0, chunks, clear_all, 0)

    peers = pieces - 1 + (j > 0).astype(jnp.int32) + (j < rows_by - 1).astype(jnp.int32)
    pl.semaphore_wait(barrier, peers)

    def remote(src, dst, send, recv, where):
        return pltpu.make_async_remote_copy(
            src_ref=src, dst_ref=dst, send_sem=send, recv_sem=recv, device_id=where, device_id_type=MESH
        )

    def east(tick, c):
        return remote(
            e_out.at[tick, c], e_in.at[tick + 1, c], e_send.at[tick, c], e_recv.at[tick, c], {"bx": i + 1}
        )

    def north(tick, c):
        return remote(
            n_out.at[tick, c], n_in.at[tick + 1, c], n_send.at[tick, c], n_recv.at[tick, c], {"by": j + 1}
        )

    def relay(c):
        return remote(
            e_out.at[TICKS - 1, c], relay_in.at[c], r_send.at[c], r_recv.at[c], {"bx": relay_to}
        )

    def difference(c):
        return remote(d_out.at[c], d_in.at[c], d_send.at[c], d_recv.at[c], {"bx": partner})

    def final_north(c):
        return remote(n_out.at[TICKS - 1, c], nf_in.at[c], nf_send.at[c], nf_recv.at[c], {"by": j + 1})

    def final_south(c):
        return remote(n_out.at[TICKS - 1, c], nb_in.at[c], nb_send.at[c], nb_recv.at[c], {"by": j - 1})

    def owner(c, o):
        if o % 2 == 1 and chunks % 2 == 0:
            return c + 1 - 2 * lax.rem(c, 2) + chunks * o
        return c + chunks * o

    def regrouped(c, o):
        return remote(
            spec.at[c, o], regroup.at[i], s_send.at[c, o], s_recv.at[i], {"bx": owner(c, o)}
        )

    def shot_rows(c, o):
        return pl.ds(pl.multiple_of(owner(c, o) * group, group), group)

    def place(part, at, size, value):
        if part == 0:
            left[at : at + size, :width] = value
            left[half + at : half + at + size, width:] = value
        else:
            left[at : at + size, width:] = -value
            left[half + at : half + at + size, :width] = value

    def product(matrix, put, loads=None, first=None, depth=None):
        for n, start in enumerate(starts):
            cols = slice(start, start + tile)
            if loads is not None:
                pl.when(first)(loads[n].wait)
            got = jnp.dot(left[...], matrix[:depth, cols], preferred_element_type=F32)
            put(cols, got.astype(BF16))

    def incident(tick, c):
        active = (first_ref[0, 0] <= tick).astype(F32)
        for part in range(2):
            for o in range(per):
                at = o * group
                rows = slice(part * half + at, part * half + at + group)
                value = (
                    e_in[tick, c, rows, :].astype(F32)
                    + n_in[tick, c, rows, :].astype(F32)
                    + active * source_ref[part, shot_rows(c, o), :].astype(F32)
                )
                place(part, at, group, value.astype(BF16))

    def arrive(tick, c):
        @pl.when(i > 0)
        def _():
            east(tick - 1, c).wait_recv()

        @pl.when(j > 0)
        def _():
            north(tick - 1, c).wait_recv()

    def sweep(step, _):
        tick, c = step // chunks, lax.rem(step, chunks)

        @pl.when(tick > 0)
        def _():
            arrive(tick, c)

        incident(tick, c)

        def put_east(cols, value):
            e_out[tick, c, :, cols] = value

        product(opx, put_east, opx_loads, step == 0)

        @pl.when(i < pieces - 1)
        def _():
            east(tick, c).start()

        def put_north(cols, value):
            n_out[tick, c, :, cols] = value

        product(opy, put_north, opy_loads, step == 0)

        @pl.when(j < rows_by - 1)
        def _():
            north(tick, c).start()

        return 0

    source_load.wait()
    lax.fori_loop(0, chunks, sweep, 0)
    tables_load.start()
    lax.fori_loop(chunks, (TICKS - 1) * chunks, sweep, 0)
    tables_load.wait()
    last = TICKS - 1

    def last_tick(c):
        arrive(last, c)
        incident(last, c)

        def put_east(cols, value):
            e_out[last, c, :, cols] = value

        product(opx, put_east)

        @pl.when(has_relay_to)
        def _():
            relay(c).start()

        def put_north(cols, value):
            n_out[last, c, :, cols] = value

        product(opy, put_north)

        @pl.when(j < rows_by - 1)
        def _():
            final_north(c).start()

        @pl.when(j > 0)
        def _():
            final_south(c).start()

    def subtract(c):
        @pl.when(has_relay_from)
        def _():
            relay(c).wait_recv()

        sign = (2 * odd - 1).astype(F32)
        d_out[c] = (sign * (relay_in[c].astype(F32) - e_out[last, c].astype(F32))).astype(BF16)
        difference(c).start()

    def reflect(c):
        difference(c).wait_recv()

        @pl.when(j > 0)
        def _():
            final_north(c).wait_recv()

        @pl.when(j < rows_by - 1)
        def _():
            final_south(c).wait_recv()

        for part in range(2):
            rows = slice(part * half, (part + 1) * half)
            value = (
                d_in[c, rows, :].astype(F32) + nf_in[c, rows, :].astype(F32) - nb_in[c, rows, :].astype(F32)
            )
            place(part, 0, half, value.astype(BF16))

        def put_reflected(cols, value):
            d_out_free[:, cols] = value

        d_out_free = e_in.at[0, c]
        product(opx, put_reflected)
        for part in range(2):
            place(part, 0, half, d_out_free[part * half : (part + 1) * half, :])

        def put_spectrum(cols, value):
            for part in range(2):
                for o in range(per):
                    at = part * half + o * group
                    if fused:
                        spec[c, o, part * group : (part + 1) * group, cols] = value[at : at + group]
                    else:
                        out_ref[part, shot_rows(c, o), cols] = value[at : at + group]

        product(tables, put_spectrum, depth=2 * width)
        if fused:
            for o in range(per):
                @pl.when(owner(c, o) == i)
                def _():
                    regroup[i] = spec[c, o]

                @pl.when(owner(c, o) != i)
                def _():
                    regrouped(c, o).start()

    def finish(step, _):
        @pl.when(step < chunks)
        def _():
            last_tick(step)

        @pl.when((step >= 1) & (step <= chunks))
        def _():
            subtract(step - 1)

        @pl.when(step >= 2)
        def _():
            reflect(step - 2)

        return 0

    lax.fori_loop(0, chunks + 2, finish, 0)

    def sent(c, _):
        for tick in range(TICKS - 1):
            @pl.when(i < pieces - 1)
            def _():
                east(tick, c).wait_send()

            @pl.when(j < rows_by - 1)
            def _():
                north(tick, c).wait_send()

        @pl.when(has_relay_to)
        def _():
            relay(c).wait_send()

        @pl.when(j < rows_by - 1)
        def _():
            final_north(c).wait_send()

        @pl.when(j > 0)
        def _():
            final_south(c).wait_send()

        difference(c).wait_send()
        return 0

    lax.fori_loop(0, chunks, sent, 0)

    if fused:
        for k in range(1, pieces):
            peer = lax.rem(i + k, pieces)
            remote(
                spec.at[0, 0], regroup.at[peer], s_send.at[0, 0], s_recv.at[peer], {"bx": peer}
            ).wait_recv()
        side = 2 * pieces * group
        whole = regroup[...].reshape(side, width)
        wave = lax.rem(lax.broadcasted_iota(jnp.int32, (side, tile), 0), pieces)
        signed = jnp.where(wave < pieces // 2, wave, wave - pieces).astype(F32)
        gain = 0.5 * (1.0 + signed / jnp.sqrt(signed * signed + 1.0))
        for start in range(0, width, tile):
            cols = slice(start, start + tile)
            got = jnp.dot(tables[2 * width :, :side], whole[:, cols], preferred_element_type=F32)
            out_ref[:, cols] = got * gain
        for c in range(chunks):
            for o in range(per):
                @pl.when(owner(c, o) != i)
                def _():
                    regrouped(c, o).wait_send()


def shards(source, start_tick, op_x, op_y):
    pieces, rows_by = lax.axis_size("bx"), lax.axis_size("by")
    _, _, _, shots, width = source.shape
    owned = shots // pieces
    fused = owned % 16 == 0 and pieces % CHUNKS == 0 and 2 * shots <= width
    per, group = (pieces // CHUNKS, owned) if fused else (1, shots // CHUNKS)
    rows = 2 * per * group
    side = 2 * pieces * owned

    cos_line, sin_line = dft_tables(width)
    tables = np.concatenate([cos_line, -sin_line])
    if fused:
        grid = np.zeros((side, width), ml_dtypes.bfloat16)
        grid[:, :side] = grid_matrix(pieces, owned)
        tables = np.concatenate([tables, grid])
    tables = jnp.asarray(tables)

    out_shape = (
        jax.ShapeDtypeStruct((side, width), F32) if fused else jax.ShapeDtypeStruct((2, shots, width), BF16)
    )
    ticked = pltpu.VMEM((TICKS, CHUNKS, rows, width), BF16)
    single = pltpu.VMEM((CHUNKS, rows, width), BF16)
    operator = pltpu.VMEM((2 * width, width), BF16)
    ticked_sem = pltpu.SemaphoreType.DMA((TICKS - 1, CHUNKS))
    single_sem = pltpu.SemaphoreType.DMA((CHUNKS,))
    result = pl.pallas_call(
        functools.partial(kernel, (pieces, rows_by, per, group, fused)),
        out_shape=out_shape,
        in_specs=[pl.BlockSpec(memory_space=pltpu.SMEM)] + [pl.BlockSpec(memory_space=pl.ANY)] * 4,
        out_specs=pl.BlockSpec(memory_space=pltpu.VMEM),
        scratch_shapes=[
            pltpu.VMEM((2, shots, width), BF16),
            operator, operator,
            pltpu.VMEM(tables.shape, BF16),
            pltpu.VMEM((rows, 2 * width), BF16),
            ticked, ticked, ticked, ticked,
            single, single, single, single, single,
            pltpu.VMEM((CHUNKS, per, 2 * group, width), BF16),
            pltpu.VMEM((pieces, 2 * group, width) if fused else (1, 16, 128), BF16),
            pltpu.SemaphoreType.DMA((2 + 2 * pl.cdiv(width, 256),)),
            ticked_sem, ticked_sem, ticked_sem, ticked_sem,
            single_sem, single_sem, single_sem, single_sem,
            single_sem, single_sem, single_sem, single_sem,
            pltpu.SemaphoreType.DMA((CHUNKS, per)),
            pltpu.SemaphoreType.DMA((pieces,)),
        ],
        compiler_params=pltpu.CompilerParams(
            collective_id=0, has_side_effects=True, vmem_limit_bytes=60 * 1024 * 1024
        ),
        cost_estimate=pl.CostEstimate(
            flops=2 * rows * CHUNKS * 2 * width * width * 10, bytes_accessed=16 * width * width, transcendentals=0
        ),
    )(
        start_tick,
        source[0, 0],
        op_x.reshape(2 * width, width),
        op_y.reshape(2 * width, width),
        tables,
    )
    if fused:
        return result.reshape(1, owned, 2, pieces, width)
    arranged = result.reshape(2, pieces, owned, 1, width)
    spectrum = lax.all_to_all(arranged, "bx", split_axis=1, concat_axis=3, tiled=True)
    received = spectrum.reshape(2, owned, pieces, width)
    cos_grid, sin_grid = (jnp.asarray(t) for t in dft_tables(pieces))

    def over_grid(values, table):
        return jnp.einsum("sik,iq->sqk", values, table, preferred_element_type=F32)

    out_real = over_grid(received[0], cos_grid) + over_grid(received[1], sin_grid)
    out_imag = over_grid(received[1], cos_grid) - over_grid(received[0], sin_grid)
    upgoing = jnp.stack([out_real, out_imag], axis=1) * grid_gain(pieces)[None, None, :, None]
    return upgoing[None]


def solution(mesh):
    placed = (
        P("bx", "by", None, None, None),
        P("bx", "by"),
        P("bx", "by", None, None, None),
        P("bx", "by", None, None, None),
    )
    return jax.shard_map(
        shards,
        mesh=mesh,
        in_specs=placed,
        out_specs=P("by", "bx", None, None, None),
        check_vma=False,
    )
```

```python
import functools
import math

import jax
import jax.numpy as jnp
import ml_dtypes
import numpy as np
from jax import lax
from jax.experimental import pallas as pl
from jax.experimental.pallas import tpu as pltpu
from jax.sharding import PartitionSpec as P

TICKS = 4
CHUNKS = 2
MESH = pl.DeviceIdType.MESH
BF16 = jnp.bfloat16
F32 = jnp.float32


def dft_tables(length):
    indices = np.arange(length, dtype=np.int64)
    angles = (indices[:, None] * indices[None, :] % length) * (2.0 * math.pi / length)
    return np.cos(angles).astype(ml_dtypes.bfloat16), np.sin(angles).astype(ml_dtypes.bfloat16)


def grid_gain(pieces):
    wave = np.arange(pieces)
    signed = np.where(wave < pieces // 2, wave, wave - pieces).astype(np.float64)
    return (0.5 * (1.0 + signed / np.sqrt(signed * signed + 1.0))).astype(np.float32)


def grid_matrix(pieces, owned):
    cos_grid, sin_grid = (t.astype(np.float32) for t in dft_tables(pieces))
    parts = np.zeros((2, pieces, pieces, 2), np.float32)
    parts[0, :, :, 0] = cos_grid.T
    parts[0, :, :, 1] = sin_grid.T
    parts[1, :, :, 0] = -sin_grid.T
    parts[1, :, :, 1] = cos_grid.T
    full = np.einsum("cqir,st->scqirt", parts, np.eye(owned, dtype=np.float32))
    side = 2 * pieces * owned
    return full.reshape(side, side).astype(ml_dtypes.bfloat16)


def kernel(
    plan,
    first_ref, source_hbm, opx_hbm, opy_hbm, tables_hbm,
    out_ref,
    source_ref, opx, opy, tables, left, e_out, n_out, e_in, n_in, relay_in, d_out, d_in, nf_in, nb_in, spec, regroup,
    load_sem, e_send, e_recv, n_send, n_recv, r_send, r_recv, d_send, d_recv,
    nf_send, nf_recv, nb_send, nb_recv, s_send, s_recv,
):
    pieces, rows_by, per, group, fused = plan
    chunks = CHUNKS
    half = per * group
    width = source_hbm.shape[2]
    tile = min(256, width)
    i, j = lax.axis_index("bx"), lax.axis_index("by")
    odd = lax.rem(i, 2)
    partner = i + 1 - 2 * odd
    relay_to = i - 2 + 4 * odd
    relay_from = i + 2 - 4 * odd
    has_relay_to = (relay_to >= 0) & (relay_to < pieces)
    has_relay_from = (relay_from >= 0) & (relay_from < pieces)

    starts = range(0, width, tile)

    def load(src, dst, k):
        return pltpu.make_async_copy(src, dst, load_sem.at[k])

    def by_tiles(src, dst, k):
        return [
            load(src.at[:, start : start + tile], dst.at[:, start : start + tile], k + n)
            for n, start in enumerate(starts)
        ]

    count = len(starts)
    source_load = load(source_hbm, source_ref, 0)
    opx_loads = by_tiles(opx_hbm, opx, 1)
    opy_loads = by_tiles(opy_hbm, opy, 1 + count)
    tables_load = load(tables_hbm, tables, 1 + 2 * count)
    for copy in [source_load, *opx_loads, *opy_loads]:
        copy.start()

    barrier = pltpu.get_barrier_semaphore()
    for k in range(1, pieces):
        pl.semaphore_signal(
            barrier, inc=1, device_id={"bx": lax.rem(i + k, pieces)}, device_id_type=MESH
        )

    @pl.when(j > 0)
    def _():
        pl.semaphore_signal(barrier, inc=1, device_id={"by": j - 1}, device_id_type=MESH)

    @pl.when(j < rows_by - 1)
    def _():
        pl.semaphore_signal(barrier, inc=1, device_id={"by": j + 1}, device_id_type=MESH)

    def clear(ref, tick, c):
        ref[tick, c] = jnp.zeros(ref.shape[2:], ref.dtype)

    def clear_all(c, _):
        clear(e_in, 0, c)
        clear(n_in, 0, c)

        @pl.when(i == 0)
        def _():
            for tick in range(1, TICKS):
                clear(e_in, tick, c)

        @pl.when(j == 0)
        def _():
            for tick in range(1, TICKS):
                clear(n_in, tick, c)
            nf_in[c] = jnp.zeros(nf_in.shape[1:], BF16)

        @pl.when(j == rows_by - 1)
        def _():
            nb_in[c] = jnp.zeros(nb_in.shape[1:], BF16)

        @pl.when(jnp.logical_not(has_relay_from))
        def _():
            relay_in[c] = jnp.zeros(relay_in.shape[1:], BF16)

        return 0

    lax.fori_loop(0, chunks, clear_all, 0)

    peers = pieces - 1 + (j > 0).astype(jnp.int32) + (j < rows_by - 1).astype(jnp.int32)
    pl.semaphore_wait(barrier, peers)

    def remote(src, dst, send, recv, where):
        return pltpu.make_async_remote_copy(
            src_ref=src, dst_ref=dst, send_sem=send, recv_sem=recv, device_id=where, device_id_type=MESH
        )

    def east(tick, c):
        return remote(
            e_out.at[tick, c], e_in.at[tick + 1, c], e_send.at[tick, c], e_recv.at[tick, c], {"bx": i + 1}
        )

    def north(tick, c):
        return remote(
            n_out.at[tick, c], n_in.at[tick + 1, c], n_send.at[tick, c], n_recv.at[tick, c], {"by": j + 1}
        )

    def relay(c):
        return remote(
            e_out.at[TICKS - 1, c], relay_in.at[c], r_send.at[c], r_recv.at[c], {"bx": relay_to}
        )

    def difference(c):
        return remote(d_out.at[c], d_in.at[c], d_send.at[c], d_recv.at[c], {"bx": partner})

    def final_north(c):
        return remote(n_out.at[TICKS - 1, c], nf_in.at[c], nf_send.at[c], nf_recv.at[c], {"by": j + 1})

    def final_south(c):
        return remote(n_out.at[TICKS - 1, c], nb_in.at[c], nb_send.at[c], nb_recv.at[c], {"by": j - 1})

    def owner(c, o):
        if o % 2 == 1 and chunks % 2 == 0:
            return c + 1 - 2 * lax.rem(c, 2) + chunks * o
        return c + chunks * o

    def regrouped(c, o):
        return remote(
            spec.at[c, o], regroup.at[i], s_send.at[c, o], s_recv.at[i], {"bx": owner(c, o)}
        )

    def shot_rows(c, o):
        return pl.ds(pl.multiple_of(owner(c, o) * group, group), group)

    def place(part, at, size, value):
        if part == 0:
            left[at : at + size, :width] = value
            left[half + at : half + at + size, width:] = value
        else:
            left[at : at + size, width:] = -value
            left[half + at : half + at + size, :width] = value

    def product(matrix, put, loads=None):
        for n, start in enumerate(starts):
            cols = slice(start, start + tile)
            if loads is not None:
                loads[n].wait()
            got = jnp.dot(left[...], matrix[:, cols], preferred_element_type=F32)
            put(cols, got.astype(BF16))

    def incident(tick, c):
        active = (first_ref[0, 0] <= tick).astype(F32)
        for part in range(2):
            for o in range(per):
                at = o * group
                rows = slice(part * half + at, part * half + at + group)
                value = (
                    e_in[tick, c, rows, :].astype(F32)
                    + n_in[tick, c, rows, :].astype(F32)
                    + active * source_ref[part, shot_rows(c, o), :].astype(F32)
                )
                place(part, at, group, value.astype(BF16))

    def arrive(tick, c):
        @pl.when(i > 0)
        def _():
            east(tick - 1, c).wait_recv()

        @pl.when(j > 0)
        def _():
            north(tick - 1, c).wait_recv()

    def sweep(step, _, first=False):
        tick, c = (0, 0) if first else (step // chunks, lax.rem(step, chunks))

        if not first:
            @pl.when(tick > 0)
            def _():
                arrive(tick, c)

        incident(tick, c)

        def put_east(cols, value):
            e_out[tick, c, :, cols] = value

        product(opx, put_east, opx_loads if first else None)

        @pl.when(i < pieces - 1)
        def _():
            east(tick, c).start()

        def put_north(cols, value):
            n_out[tick, c, :, cols] = value

        product(opy, put_north, opy_loads if first else None)

        @pl.when(j < rows_by - 1)
        def _():
            north(tick, c).start()

        return 0

    source_load.wait()
    sweep(0, 0, first=True)
    tables_load.start()
    lax.fori_loop(1, (TICKS - 1) * chunks, sweep, 0)
    tables_load.wait()
    last = TICKS - 1

    def last_tick(c):
        arrive(last, c)
        incident(last, c)

        def put_east(cols, value):
            e_out[last, c, :, cols] = value

        product(opx, put_east)

        @pl.when(has_relay_to)
        def _():
            relay(c).start()

        def put_north(cols, value):
            n_out[last, c, :, cols] = value

        product(opy, put_north)

        @pl.when(j < rows_by - 1)
        def _():
            final_north(c).start()

        @pl.when(j > 0)
        def _():
            final_south(c).start()

    def subtract(c):
        @pl.when(has_relay_from)
        def _():
            relay(c).wait_recv()

        sign = (2 * odd - 1).astype(F32)
        d_out[c] = (sign * (relay_in[c].astype(F32) - e_out[last, c].astype(F32))).astype(BF16)
        difference(c).start()

    def reflect(c):
        difference(c).wait_recv()

        @pl.when(j > 0)
        def _():
            final_north(c).wait_recv()

        @pl.when(j < rows_by - 1)
        def _():
            final_south(c).wait_recv()

        for part in range(2):
            rows = slice(part * half, (part + 1) * half)
            value = (
                d_in[c, rows, :].astype(F32) + nf_in[c, rows, :].astype(F32) - nb_in[c, rows, :].astype(F32)
            )
            place(part, 0, half, value.astype(BF16))

        def put_reflected(cols, value):
            d_out_free[:, cols] = value

        d_out_free = e_in.at[0, c]
        product(opx, put_reflected)
        for part in range(2):
            place(part, 0, half, d_out_free[part * half : (part + 1) * half, :])

        def put_spectrum(cols, value):
            for part in range(2):
                for o in range(per):
                    at = part * half + o * group
                    if fused:
                        spec[c, o, part * group : (part + 1) * group, cols] = value[at : at + group]
                    else:
                        out_ref[part, shot_rows(c, o), cols] = value[at : at + group]

        product(tables, put_spectrum)
        if fused:
            for o in range(per):
                @pl.when(owner(c, o) == i)
                def _():
                    regroup[i] = spec[c, o]

                @pl.when(owner(c, o) != i)
                def _():
                    regrouped(c, o).start()

    def finish(step, _):
        @pl.when(step < chunks)
        def _():
            last_tick(step)

        @pl.when((step >= 1) & (step <= chunks))
        def _():
            subtract(step - 1)

        @pl.when(step >= 2)
        def _():
            reflect(step - 2)

        return 0

    lax.fori_loop(0, chunks + 2, finish, 0)

    def sent(c, _):
        for tick in range(TICKS - 1):
            @pl.when(i < pieces - 1)
            def _():
                east(tick, c).wait_send()

            @pl.when(j < rows_by - 1)
            def _():
                north(tick, c).wait_send()

        @pl.when(has_relay_to)
        def _():
            relay(c).wait_send()

        @pl.when(j < rows_by - 1)
        def _():
            final_north(c).wait_send()

        @pl.when(j > 0)
        def _():
            final_south(c).wait_send()

        difference(c).wait_send()
        return 0

    lax.fori_loop(0, chunks, sent, 0)

    if fused:
        for k in range(1, pieces):
            peer = lax.rem(i + k, pieces)
            remote(
                spec.at[0, 0], regroup.at[peer], s_send.at[0, 0], s_recv.at[peer], {"bx": peer}
            ).wait_recv()
        out_ref[...] = regroup[...]
        for c in range(chunks):
            for o in range(per):
                @pl.when(owner(c, o) != i)
                def _():
                    regrouped(c, o).wait_send()


def shards(source, start_tick, op_x, op_y):
    pieces, rows_by = lax.axis_size("bx"), lax.axis_size("by")
    _, _, _, shots, width = source.shape
    owned = shots // pieces
    fused = owned % 16 == 0 and pieces % CHUNKS == 0
    per, group = (pieces // CHUNKS, owned) if fused else (1, shots // CHUNKS)
    rows = 2 * per * group
    side = 2 * pieces * owned

    cos_line, sin_line = dft_tables(width)
    tables = jnp.asarray(np.concatenate([cos_line, -sin_line]))

    out_shape = (
        jax.ShapeDtypeStruct((pieces, 2 * owned, width), BF16) if fused else jax.ShapeDtypeStruct((2, shots, width), BF16)
    )
    ticked = pltpu.VMEM((TICKS, CHUNKS, rows, width), BF16)
    single = pltpu.VMEM((CHUNKS, rows, width), BF16)
    operator = pltpu.VMEM((2 * width, width), BF16)
    ticked_sem = pltpu.SemaphoreType.DMA((TICKS - 1, CHUNKS))
    single_sem = pltpu.SemaphoreType.DMA((CHUNKS,))
    result = pl.pallas_call(
        functools.partial(kernel, (pieces, rows_by, per, group, fused)),
        out_shape=out_shape,
        in_specs=[pl.BlockSpec(memory_space=pltpu.SMEM)] + [pl.BlockSpec(memory_space=pl.ANY)] * 4,
        out_specs=pl.BlockSpec(memory_space=pltpu.VMEM),
        scratch_shapes=[
            pltpu.VMEM((2, shots, width), BF16),
            operator, operator,
            pltpu.VMEM(tables.shape, BF16),
            pltpu.VMEM((rows, 2 * width), BF16),
            ticked, ticked, ticked, ticked,
            single, single, single, single, single,
            pltpu.VMEM((CHUNKS, per, 2 * group, width), BF16),
            pltpu.VMEM((pieces, 2 * group, width) if fused else (1, 16, 128), BF16),
            pltpu.SemaphoreType.DMA((2 + 2 * pl.cdiv(width, 256),)),
            ticked_sem, ticked_sem, ticked_sem, ticked_sem,
            single_sem, single_sem, single_sem, single_sem,
            single_sem, single_sem, single_sem, single_sem,
            pltpu.SemaphoreType.DMA((CHUNKS, per)),
            pltpu.SemaphoreType.DMA((pieces,)),
        ],
        compiler_params=pltpu.CompilerParams(
            collective_id=0, has_side_effects=True, vmem_limit_bytes=60 * 1024 * 1024
        ),
        cost_estimate=pl.CostEstimate(
            flops=2 * rows * CHUNKS * 2 * width * width * 10, bytes_accessed=16 * width * width, transcendentals=0
        ),
    )(
        start_tick,
        source[0, 0],
        op_x.reshape(2 * width, width),
        op_y.reshape(2 * width, width),
        tables,
    )
    if fused:
        grid = jnp.asarray(grid_matrix(pieces, owned))
        gain = jnp.asarray(np.tile(grid_gain(pieces), 2 * owned))
        upgoing = jnp.dot(grid, result.reshape(side, width), preferred_element_type=F32) * gain[:, None]
        return upgoing.reshape(1, owned, 2, pieces, width)
    arranged = result.reshape(2, pieces, owned, 1, width)
    spectrum = lax.all_to_all(arranged, "bx", split_axis=1, concat_axis=3, tiled=True)
    received = spectrum.reshape(2, owned, pieces, width)
    cos_grid, sin_grid = (jnp.asarray(t) for t in dft_tables(pieces))

    def over_grid(values, table):
        return jnp.einsum("sik,iq->sqk", values, table, preferred_element_type=F32)

    out_real = over_grid(received[0], cos_grid) + over_grid(received[1], sin_grid)
    out_imag = over_grid(received[1], cos_grid) - over_grid(received[0], sin_grid)
    upgoing = jnp.stack([out_real, out_imag], axis=1) * grid_gain(pieces)[None, None, :, None]
    return upgoing[None]


def solution(mesh):
    placed = (
        P("bx", "by", None, None, None),
        P("bx", "by"),
        P("bx", "by", None, None, None),
        P("bx", "by", None, None, None),
    )
    return jax.shard_map(
        shards,
        mesh=mesh,
        in_specs=placed,
        out_specs=P("by", "bx", None, None, None),
        check_vma=False,
    )
```

```python
import functools
import math

import jax
import jax.numpy as jnp
import ml_dtypes
import numpy as np
from jax import lax
from jax.experimental import pallas as pl
from jax.experimental.pallas import tpu as pltpu
from jax.sharding import PartitionSpec as P

TICKS = 4
CHUNKS = 2
MESH = pl.DeviceIdType.MESH
BF16 = jnp.bfloat16
F32 = jnp.float32


def dft_tables(length):
    indices = np.arange(length, dtype=np.int64)
    angles = (indices[:, None] * indices[None, :] % length) * (2.0 * math.pi / length)
    return np.cos(angles).astype(ml_dtypes.bfloat16), np.sin(angles).astype(ml_dtypes.bfloat16)


def grid_gain(pieces):
    wave = np.arange(pieces)
    signed = np.where(wave < pieces // 2, wave, wave - pieces).astype(np.float64)
    return (0.5 * (1.0 + signed / np.sqrt(signed * signed + 1.0))).astype(np.float32)


def grid_matrix(pieces, owned):
    cos_grid, sin_grid = (t.astype(np.float32) for t in dft_tables(pieces))
    parts = np.zeros((2, pieces, pieces, 2), np.float32)
    parts[0, :, :, 0] = cos_grid.T
    parts[0, :, :, 1] = sin_grid.T
    parts[1, :, :, 0] = -sin_grid.T
    parts[1, :, :, 1] = cos_grid.T
    full = np.einsum("cqir,st->scqirt", parts, np.eye(owned, dtype=np.float32))
    side = 2 * pieces * owned
    return full.reshape(side, side).astype(ml_dtypes.bfloat16)


def kernel(
    plan,
    first_ref, source_hbm, opx_hbm, opy_hbm, tables_hbm,
    out_ref,
    source_ref, opx, opy, tables, left, e_out, n_out, e_in, n_in, relay_in, d_out, d_in, nf_in, nb_in, spec, regroup,
    load_sem, e_send, e_recv, n_send, n_recv, r_send, r_recv, d_send, d_recv,
    nf_send, nf_recv, nb_send, nb_recv, s_send, s_recv,
):
    pieces, rows_by, per, group, fused, spans = plan
    chunks = CHUNKS
    half = per * group
    width = source_hbm.shape[2]
    tile = min(256, width)
    i, j = lax.axis_index("bx"), lax.axis_index("by")
    odd = lax.rem(i, 2)
    partner = i + 1 - 2 * odd
    relay_to = i - 2 + 4 * odd
    relay_from = i + 2 - 4 * odd
    has_relay_to = (relay_to >= 0) & (relay_to < pieces)
    has_relay_from = (relay_from >= 0) & (relay_from < pieces)

    starts = range(0, width, tile)

    def load(src, dst, k):
        return pltpu.make_async_copy(src, dst, load_sem.at[k])

    def by_tiles(src, dst, k):
        return [
            load(src.at[:, start : start + tile], dst.at[:, start : start + tile], k + n)
            for n, start in enumerate(starts)
        ]

    count = len(starts)
    span = width // spans
    source_load = load(source_hbm, source_ref, 0)
    opx_loads = by_tiles(opx_hbm, opx, 1)
    opy_loads = by_tiles(opy_hbm, opy, 1 + count)
    tables_load = load(tables_hbm, tables, 1 + 2 * count)
    for copy in [source_load, *opx_loads, *opy_loads]:
        copy.start()

    barrier = pltpu.get_barrier_semaphore()
    for k in range(1, pieces):
        pl.semaphore_signal(
            barrier, inc=1, device_id={"bx": lax.rem(i + k, pieces)}, device_id_type=MESH
        )

    @pl.when(j > 0)
    def _():
        pl.semaphore_signal(barrier, inc=1, device_id={"by": j - 1}, device_id_type=MESH)

    @pl.when(j < rows_by - 1)
    def _():
        pl.semaphore_signal(barrier, inc=1, device_id={"by": j + 1}, device_id_type=MESH)

    def clear(ref, tick, c):
        ref[tick, c] = jnp.zeros(ref.shape[2:], ref.dtype)

    def clear_all(c, _):
        clear(e_in, 0, c)
        clear(n_in, 0, c)

        @pl.when(i == 0)
        def _():
            for tick in range(1, TICKS):
                clear(e_in, tick, c)

        @pl.when(j == 0)
        def _():
            for tick in range(1, TICKS):
                clear(n_in, tick, c)
            nf_in[c] = jnp.zeros(nf_in.shape[1:], BF16)

        @pl.when(j == rows_by - 1)
        def _():
            nb_in[c] = jnp.zeros(nb_in.shape[1:], BF16)

        @pl.when(jnp.logical_not(has_relay_from))
        def _():
            relay_in[c] = jnp.zeros(relay_in.shape[1:], BF16)

        return 0

    lax.fori_loop(0, chunks, clear_all, 0)

    peers = pieces - 1 + (j > 0).astype(jnp.int32) + (j < rows_by - 1).astype(jnp.int32)
    pl.semaphore_wait(barrier, peers)

    def remote(src, dst, send, recv, where):
        return pltpu.make_async_remote_copy(
            src_ref=src, dst_ref=dst, send_sem=send, recv_sem=recv, device_id=where, device_id_type=MESH
        )

    def east(tick, c):
        return remote(
            e_out.at[tick, c], e_in.at[tick + 1, c], e_send.at[tick, c], e_recv.at[tick, c], {"bx": i + 1}
        )

    def north(tick, c):
        return remote(
            n_out.at[tick, c], n_in.at[tick + 1, c], n_send.at[tick, c], n_recv.at[tick, c], {"by": j + 1}
        )

    def relay(c, n):
        cols = pl.ds(starts[n], tile)
        return remote(
            e_out.at[TICKS - 1, c, :, cols], relay_in.at[c, :, cols], r_send.at[c, n], r_recv.at[c, n],
            {"bx": relay_to},
        )

    def difference(c, n):
        cols = pl.ds(starts[n], tile)
        return remote(
            d_out.at[c, :, cols], d_in.at[c, :, cols], d_send.at[c, n], d_recv.at[c, n], {"bx": partner}
        )

    def final_north(c):
        return remote(n_out.at[TICKS - 1, c], nf_in.at[c], nf_send.at[c], nf_recv.at[c], {"by": j + 1})

    def final_south(c):
        return remote(n_out.at[TICKS - 1, c], nb_in.at[c], nb_send.at[c], nb_recv.at[c], {"by": j - 1})

    def owner(c, o):
        if o % 2 == 1 and chunks % 2 == 0:
            return c + 1 - 2 * lax.rem(c, 2) + chunks * o
        return c + chunks * o

    def regrouped(c, o, part):
        cols = pl.ds(part * span, span)
        return remote(
            spec.at[c, o, :, cols], regroup.at[i, :, cols], s_send.at[c, o, part], s_recv.at[i, part],
            {"bx": owner(c, o)},
        )

    def shot_rows(c, o):
        return pl.ds(pl.multiple_of(owner(c, o) * group, group), group)

    def place(part, at, size, value):
        if part == 0:
            left[at : at + size, :width] = value
            left[half + at : half + at + size, width:] = value
        else:
            left[at : at + size, width:] = -value
            left[half + at : half + at + size, :width] = value

    def product(matrix, put, loads=None, then=None):
        for n, start in enumerate(starts):
            cols = slice(start, start + tile)
            if loads is not None:
                loads[n].wait()
            got = jnp.dot(left[...], matrix[:, cols], preferred_element_type=F32)
            put(cols, got.astype(BF16))
            if then is not None:
                then(n)

    def incident(tick, c):
        active = (first_ref[0, 0] <= tick).astype(F32)
        for part in range(2):
            for o in range(per):
                at = o * group
                rows = slice(part * half + at, part * half + at + group)
                value = (
                    e_in[tick, c, rows, :].astype(F32)
                    + n_in[tick, c, rows, :].astype(F32)
                    + active * source_ref[part, shot_rows(c, o), :].astype(F32)
                )
                place(part, at, group, value.astype(BF16))

    def arrive(tick, c):
        @pl.when(i > 0)
        def _():
            east(tick - 1, c).wait_recv()

        @pl.when(j > 0)
        def _():
            north(tick - 1, c).wait_recv()

    def sweep(step, _, first=False):
        tick, c = (0, 0) if first else (step // chunks, lax.rem(step, chunks))

        if not first:
            @pl.when(tick > 0)
            def _():
                arrive(tick, c)

        incident(tick, c)

        def put_east(cols, value):
            e_out[tick, c, :, cols] = value

        product(opx, put_east, opx_loads if first else None)

        @pl.when(i < pieces - 1)
        def _():
            east(tick, c).start()

        def put_north(cols, value):
            n_out[tick, c, :, cols] = value

        product(opy, put_north, opy_loads if first else None)

        @pl.when(j < rows_by - 1)
        def _():
            north(tick, c).start()

        return 0

    source_load.wait()
    sweep(0, 0, first=True)
    tables_load.start()
    lax.fori_loop(1, (TICKS - 1) * chunks, sweep, 0)
    tables_load.wait()
    last = TICKS - 1

    def last_tick(c):
        arrive(last, c)
        incident(last, c)

        def put_east(cols, value):
            e_out[last, c, :, cols] = value

        def send_east(n):
            @pl.when(has_relay_to)
            def _():
                relay(c, n).start()

        product(opx, put_east, then=send_east)

        def put_north(cols, value):
            n_out[last, c, :, cols] = value

        product(opy, put_north)

        @pl.when(j < rows_by - 1)
        def _():
            final_north(c).start()

        @pl.when(j > 0)
        def _():
            final_south(c).start()

    def subtract(c):
        sign = (2 * odd - 1).astype(F32)
        for n, start in enumerate(starts):
            @pl.when(has_relay_from)
            def _():
                relay(c, n).wait_recv()

            cols = slice(start, start + tile)
            value = relay_in[c, :, cols].astype(F32) - e_out[last, c, :, cols].astype(F32)
            d_out[c, :, cols] = (sign * value).astype(BF16)
            difference(c, n).start()

    def reflect(c):
        for n in range(count):
            difference(c, n).wait_recv()

        @pl.when(j > 0)
        def _():
            final_north(c).wait_recv()

        @pl.when(j < rows_by - 1)
        def _():
            final_south(c).wait_recv()

        for part in range(2):
            rows = slice(part * half, (part + 1) * half)
            value = (
                d_in[c, rows, :].astype(F32) + nf_in[c, rows, :].astype(F32) - nb_in[c, rows, :].astype(F32)
            )
            place(part, 0, half, value.astype(BF16))

        def put_reflected(cols, value):
            d_out_free[:, cols] = value

        d_out_free = e_in.at[0, c]
        product(opx, put_reflected)
        for part in range(2):
            place(part, 0, half, d_out_free[part * half : (part + 1) * half, :])

        def put_spectrum(cols, value):
            for part in range(2):
                for o in range(per):
                    at = part * half + o * group
                    if fused:
                        spec[c, o, part * group : (part + 1) * group, cols] = value[at : at + group]
                    else:
                        out_ref[part, shot_rows(c, o), cols] = value[at : at + group]

        def send_spectrum(n):
            if not fused or (n + 1) * spans % count:
                return
            part = (n + 1) * spans // count - 1
            cols = slice(part * span, (part + 1) * span)
            for o in range(per):
                @pl.when(owner(c, o) == i)
                def _():
                    regroup[i, :, cols] = spec[c, o, :, cols]

                @pl.when(owner(c, o) != i)
                def _():
                    regrouped(c, o, part).start()

        product(tables, put_spectrum, then=send_spectrum)

    def finish(step, _):
        @pl.when(step < chunks)
        def _():
            last_tick(step)

        @pl.when((step >= 1) & (step <= chunks))
        def _():
            subtract(step - 1)

        @pl.when(step >= 2)
        def _():
            reflect(step - 2)

        return 0

    lax.fori_loop(0, chunks + 2, finish, 0)

    def sent(c, _):
        for tick in range(TICKS - 1):
            @pl.when(i < pieces - 1)
            def _():
                east(tick, c).wait_send()

            @pl.when(j < rows_by - 1)
            def _():
                north(tick, c).wait_send()

        for n in range(count):
            @pl.when(has_relay_to)
            def _():
                relay(c, n).wait_send()

            difference(c, n).wait_send()

        @pl.when(j < rows_by - 1)
        def _():
            final_north(c).wait_send()

        @pl.when(j > 0)
        def _():
            final_south(c).wait_send()

        return 0

    lax.fori_loop(0, chunks, sent, 0)

    if fused:
        for k in range(1, pieces):
            peer = lax.rem(i + k, pieces)
            for part in range(spans):
                cols = pl.ds(part * span, span)
                remote(
                    spec.at[0, 0, :, cols], regroup.at[peer, :, cols], s_send.at[0, 0, part],
                    s_recv.at[peer, part], {"bx": peer},
                ).wait_recv()
        out_ref[...] = regroup[...]
        for c in range(chunks):
            for o in range(per):
                @pl.when(owner(c, o) != i)
                def _():
                    for part in range(spans):
                        regrouped(c, o, part).wait_send()


def shards(source, start_tick, op_x, op_y):
    pieces, rows_by = lax.axis_size("bx"), lax.axis_size("by")
    _, _, _, shots, width = source.shape
    owned = shots // pieces
    fused = owned % 16 == 0 and pieces % CHUNKS == 0
    per, group = (pieces // CHUNKS, owned) if fused else (1, shots // CHUNKS)
    rows = 2 * per * group
    side = 2 * pieces * owned

    cos_line, sin_line = dft_tables(width)
    tables = jnp.asarray(np.concatenate([cos_line, -sin_line]))

    out_shape = (
        jax.ShapeDtypeStruct((pieces, 2 * owned, width), BF16) if fused else jax.ShapeDtypeStruct((2, shots, width), BF16)
    )
    ticked = pltpu.VMEM((TICKS, CHUNKS, rows, width), BF16)
    single = pltpu.VMEM((CHUNKS, rows, width), BF16)
    operator = pltpu.VMEM((2 * width, width), BF16)
    ticked_sem = pltpu.SemaphoreType.DMA((TICKS - 1, CHUNKS))
    tiles = pl.cdiv(width, 256)
    spans = 2 if tiles % 2 == 0 else 1
    tiled_sem = pltpu.SemaphoreType.DMA((CHUNKS, tiles))
    single_sem = pltpu.SemaphoreType.DMA((CHUNKS,))
    result = pl.pallas_call(
        functools.partial(kernel, (pieces, rows_by, per, group, fused, spans)),
        out_shape=out_shape,
        in_specs=[pl.BlockSpec(memory_space=pltpu.SMEM)] + [pl.BlockSpec(memory_space=pl.ANY)] * 4,
        out_specs=pl.BlockSpec(memory_space=pltpu.VMEM),
        scratch_shapes=[
            pltpu.VMEM((2, shots, width), BF16),
            operator, operator,
            pltpu.VMEM(tables.shape, BF16),
            pltpu.VMEM((rows, 2 * width), BF16),
            ticked, ticked, ticked, ticked,
            single, single, single, single, single,
            pltpu.VMEM((CHUNKS, per, 2 * group, width), BF16),
            pltpu.VMEM((pieces, 2 * group, width) if fused else (1, 16, 128), BF16),
            pltpu.SemaphoreType.DMA((2 + 2 * tiles,)),
            ticked_sem, ticked_sem, ticked_sem, ticked_sem,
            tiled_sem, tiled_sem, tiled_sem, tiled_sem,
            single_sem, single_sem, single_sem, single_sem,
            pltpu.SemaphoreType.DMA((CHUNKS, per, spans)),
            pltpu.SemaphoreType.DMA((pieces, spans)),
        ],
        compiler_params=pltpu.CompilerParams(
            collective_id=0, has_side_effects=True, vmem_limit_bytes=60 * 1024 * 1024
        ),
        cost_estimate=pl.CostEstimate(
            flops=2 * rows * CHUNKS * 2 * width * width * 10, bytes_accessed=16 * width * width, transcendentals=0
        ),
    )(
        start_tick,
        source[0, 0],
        op_x.reshape(2 * width, width),
        op_y.reshape(2 * width, width),
        tables,
    )
    if fused:
        grid = jnp.asarray(grid_matrix(pieces, owned))
        gain = jnp.asarray(np.tile(grid_gain(pieces), 2 * owned))
        upgoing = jnp.dot(grid, result.reshape(side, width), preferred_element_type=F32) * gain[:, None]
        return upgoing.reshape(1, owned, 2, pieces, width)
    arranged = result.reshape(2, pieces, owned, 1, width)
    spectrum = lax.all_to_all(arranged, "bx", split_axis=1, concat_axis=3, tiled=True)
    received = spectrum.reshape(2, owned, pieces, width)
    cos_grid, sin_grid = (jnp.asarray(t) for t in dft_tables(pieces))

    def over_grid(values, table):
        return jnp.einsum("sik,iq->sqk", values, table, preferred_element_type=F32)

    out_real = over_grid(received[0], cos_grid) + over_grid(received[1], sin_grid)
    out_imag = over_grid(received[1], cos_grid) - over_grid(received[0], sin_grid)
    upgoing = jnp.stack([out_real, out_imag], axis=1) * grid_gain(pieces)[None, None, :, None]
    return upgoing[None]


def solution(mesh):
    placed = (
        P("bx", "by", None, None, None),
        P("bx", "by"),
        P("bx", "by", None, None, None),
        P("bx", "by", None, None, None),
    )
    return jax.shard_map(
        shards,
        mesh=mesh,
        in_specs=placed,
        out_specs=P("by", "bx", None, None, None),
        check_vma=False,
    )
```

```python
import functools
import math

import jax
import jax.numpy as jnp
import ml_dtypes
import numpy as np
from jax import lax
from jax.experimental import pallas as pl
from jax.experimental.pallas import tpu as pltpu
from jax.sharding import PartitionSpec as P

TICKS = 4
CHUNKS = 4
MESH = pl.DeviceIdType.MESH
BF16 = jnp.bfloat16
F32 = jnp.float32


def dft_tables(length):
    indices = np.arange(length, dtype=np.int64)
    angles = (indices[:, None] * indices[None, :] % length) * (2.0 * math.pi / length)
    return np.cos(angles).astype(ml_dtypes.bfloat16), np.sin(angles).astype(ml_dtypes.bfloat16)


def grid_gain(pieces):
    wave = np.arange(pieces)
    signed = np.where(wave < pieces // 2, wave, wave - pieces).astype(np.float64)
    return (0.5 * (1.0 + signed / np.sqrt(signed * signed + 1.0))).astype(np.float32)


def grid_matrix(pieces, owned):
    cos_grid, sin_grid = (t.astype(np.float32) for t in dft_tables(pieces))
    parts = np.zeros((2, pieces, pieces, 2), np.float32)
    parts[0, :, :, 0] = cos_grid.T
    parts[0, :, :, 1] = sin_grid.T
    parts[1, :, :, 0] = -sin_grid.T
    parts[1, :, :, 1] = cos_grid.T
    full = np.einsum("cqir,st->scqirt", parts, np.eye(owned, dtype=np.float32))
    side = 2 * pieces * owned
    return full.reshape(side, side).astype(ml_dtypes.bfloat16)


def kernel(
    plan,
    first_ref, source_hbm, opx_hbm, opy_hbm, tables_hbm,
    out_ref,
    source_ref, opx, opy, tables, left, e_out, n_out, e_in, n_in, relay_in, d_out, d_in, nf_in, nb_in, spec, regroup,
    load_sem, e_send, e_recv, n_send, n_recv, r_send, r_recv, d_send, d_recv,
    nf_send, nf_recv, nb_send, nb_recv, s_send, s_recv,
):
    pieces, rows_by, per, group, fused, spans = plan
    chunks = CHUNKS
    half = per * group
    width = source_hbm.shape[2]
    tile = min(256, width)
    i, j = lax.axis_index("bx"), lax.axis_index("by")
    odd = lax.rem(i, 2)
    partner = i + 1 - 2 * odd
    relay_to = i - 2 + 4 * odd
    relay_from = i + 2 - 4 * odd
    has_relay_to = (relay_to >= 0) & (relay_to < pieces)
    has_relay_from = (relay_from >= 0) & (relay_from < pieces)

    starts = range(0, width, tile)

    def load(src, dst, k):
        return pltpu.make_async_copy(src, dst, load_sem.at[k])

    def by_tiles(src, dst, k):
        return [
            load(src.at[:, start : start + tile], dst.at[:, start : start + tile], k + n)
            for n, start in enumerate(starts)
        ]

    count = len(starts)
    span = width // spans
    source_load = load(source_hbm, source_ref, 0)
    opx_loads = by_tiles(opx_hbm, opx, 1)
    opy_loads = by_tiles(opy_hbm, opy, 1 + count)
    tables_load = load(tables_hbm, tables, 1 + 2 * count)
    for copy in [source_load, *opx_loads, *opy_loads]:
        copy.start()

    barrier = pltpu.get_barrier_semaphore()
    for k in range(1, pieces):
        pl.semaphore_signal(
            barrier, inc=1, device_id={"bx": lax.rem(i + k, pieces)}, device_id_type=MESH
        )

    @pl.when(j > 0)
    def _():
        pl.semaphore_signal(barrier, inc=1, device_id={"by": j - 1}, device_id_type=MESH)

    @pl.when(j < rows_by - 1)
    def _():
        pl.semaphore_signal(barrier, inc=1, device_id={"by": j + 1}, device_id_type=MESH)

    def clear(ref, tick, c):
        ref[tick, c] = jnp.zeros(ref.shape[2:], ref.dtype)

    def clear_all(c, _):
        clear(e_in, 0, c)
        clear(n_in, 0, c)

        @pl.when(i == 0)
        def _():
            for tick in range(1, TICKS):
                clear(e_in, tick, c)

        @pl.when(j == 0)
        def _():
            for tick in range(1, TICKS):
                clear(n_in, tick, c)
            nf_in[c] = jnp.zeros(nf_in.shape[1:], BF16)

        @pl.when(j == rows_by - 1)
        def _():
            nb_in[c] = jnp.zeros(nb_in.shape[1:], BF16)

        @pl.when(jnp.logical_not(has_relay_from))
        def _():
            relay_in[c] = jnp.zeros(relay_in.shape[1:], BF16)

        return 0

    lax.fori_loop(0, chunks, clear_all, 0)

    peers = pieces - 1 + (j > 0).astype(jnp.int32) + (j < rows_by - 1).astype(jnp.int32)
    pl.semaphore_wait(barrier, peers)

    def remote(src, dst, send, recv, where):
        return pltpu.make_async_remote_copy(
            src_ref=src, dst_ref=dst, send_sem=send, recv_sem=recv, device_id=where, device_id_type=MESH
        )

    def east(tick, c):
        return remote(
            e_out.at[tick, c], e_in.at[tick + 1, c], e_send.at[tick, c], e_recv.at[tick, c], {"bx": i + 1}
        )

    def north(tick, c):
        return remote(
            n_out.at[tick, c], n_in.at[tick + 1, c], n_send.at[tick, c], n_recv.at[tick, c], {"by": j + 1}
        )

    def relay(c, n):
        cols = pl.ds(starts[n], tile)
        return remote(
            e_out.at[TICKS - 1, c, :, cols], relay_in.at[c, :, cols], r_send.at[c, n], r_recv.at[c, n],
            {"bx": relay_to},
        )

    def difference(c, n):
        cols = pl.ds(starts[n], tile)
        return remote(
            d_out.at[c, :, cols], d_in.at[c, :, cols], d_send.at[c, n], d_recv.at[c, n], {"bx": partner}
        )

    def final_north(c):
        return remote(n_out.at[TICKS - 1, c], nf_in.at[c], nf_send.at[c], nf_recv.at[c], {"by": j + 1})

    def final_south(c):
        return remote(n_out.at[TICKS - 1, c], nb_in.at[c], nb_send.at[c], nb_recv.at[c], {"by": j - 1})

    def owner(c, o):
        if o % 2 == 1 and chunks % 2 == 0:
            return c + 1 - 2 * lax.rem(c, 2) + chunks * o
        return c + chunks * o

    def regrouped(c, o, part):
        cols = pl.ds(part * span, span)
        return remote(
            spec.at[c, o, :, cols], regroup.at[i, :, cols], s_send.at[c, o, part], s_recv.at[i, part],
            {"bx": owner(c, o)},
        )

    def shot_rows(c, o):
        return pl.ds(pl.multiple_of(owner(c, o) * group, group), group)

    def place(part, at, size, value):
        if part == 0:
            left[at : at + size, :width] = value
            left[half + at : half + at + size, width:] = value
        else:
            left[at : at + size, width:] = -value
            left[half + at : half + at + size, :width] = value

    def product(matrix, put, loads=None, then=None):
        for n, start in enumerate(starts):
            cols = slice(start, start + tile)
            if loads is not None:
                loads[n].wait()
            got = jnp.dot(left[...], matrix[:, cols], preferred_element_type=F32)
            put(cols, got.astype(BF16))
            if then is not None:
                then(n)

    def incident(tick, c):
        active = (first_ref[0, 0] <= tick).astype(F32)
        for part in range(2):
            for o in range(per):
                at = o * group
                rows = slice(part * half + at, part * half + at + group)
                value = (
                    e_in[tick, c, rows, :].astype(F32)
                    + n_in[tick, c, rows, :].astype(F32)
                    + active * source_ref[part, shot_rows(c, o), :].astype(F32)
                )
                place(part, at, group, value.astype(BF16))

    def arrive(tick, c):
        @pl.when(i > 0)
        def _():
            east(tick - 1, c).wait_recv()

        @pl.when(j > 0)
        def _():
            north(tick - 1, c).wait_recv()

    def sweep(step, _, first=False):
        tick, c = (0, 0) if first else (step // chunks, lax.rem(step, chunks))

        if not first:
            @pl.when(tick > 0)
            def _():
                arrive(tick, c)

        incident(tick, c)

        def put_east(cols, value):
            e_out[tick, c, :, cols] = value

        product(opx, put_east, opx_loads if first else None)

        @pl.when(i < pieces - 1)
        def _():
            east(tick, c).start()

        def put_north(cols, value):
            n_out[tick, c, :, cols] = value

        product(opy, put_north, opy_loads if first else None)

        @pl.when(j < rows_by - 1)
        def _():
            north(tick, c).start()

        return 0

    source_load.wait()
    sweep(0, 0, first=True)
    tables_load.start()
    lax.fori_loop(1, (TICKS - 1) * chunks, sweep, 0)
    tables_load.wait()
    last = TICKS - 1

    def last_tick(c):
        arrive(last, c)
        incident(last, c)

        def put_east(cols, value):
            e_out[last, c, :, cols] = value

        def send_east(n):
            @pl.when(has_relay_to)
            def _():
                relay(c, n).start()

        product(opx, put_east, then=send_east)

        def put_north(cols, value):
            n_out[last, c, :, cols] = value

        product(opy, put_north)

        @pl.when(j < rows_by - 1)
        def _():
            final_north(c).start()

        @pl.when(j > 0)
        def _():
            final_south(c).start()

    def subtract(c):
        sign = (2 * odd - 1).astype(F32)
        for n, start in enumerate(starts):
            @pl.when(has_relay_from)
            def _():
                relay(c, n).wait_recv()

            cols = slice(start, start + tile)
            value = relay_in[c, :, cols].astype(F32) - e_out[last, c, :, cols].astype(F32)
            d_out[c, :, cols] = (sign * value).astype(BF16)
            difference(c, n).start()

    def reflect(c):
        for n in range(count):
            difference(c, n).wait_recv()

        @pl.when(j > 0)
        def _():
            final_north(c).wait_recv()

        @pl.when(j < rows_by - 1)
        def _():
            final_south(c).wait_recv()

        for part in range(2):
            rows = slice(part * half, (part + 1) * half)
            value = (
                d_in[c, rows, :].astype(F32) + nf_in[c, rows, :].astype(F32) - nb_in[c, rows, :].astype(F32)
            )
            place(part, 0, half, value.astype(BF16))

        def put_reflected(cols, value):
            d_out_free[:, cols] = value

        d_out_free = e_in.at[0, c]
        product(opx, put_reflected)
        for part in range(2):
            place(part, 0, half, d_out_free[part * half : (part + 1) * half, :])

        def put_spectrum(cols, value):
            for part in range(2):
                for o in range(per):
                    at = part * half + o * group
                    if fused:
                        spec[c, o, part * group : (part + 1) * group, cols] = value[at : at + group]
                    else:
                        out_ref[part, shot_rows(c, o), cols] = value[at : at + group]

        def send_spectrum(n):
            if not fused or (n + 1) * spans % count:
                return
            part = (n + 1) * spans // count - 1
            cols = slice(part * span, (part + 1) * span)
            for o in range(per):
                @pl.when(owner(c, o) == i)
                def _():
                    regroup[i, :, cols] = spec[c, o, :, cols]

                @pl.when(owner(c, o) != i)
                def _():
                    regrouped(c, o, part).start()

        product(tables, put_spectrum, then=send_spectrum)

    def finish(step, _):
        @pl.when(step < chunks)
        def _():
            last_tick(step)

        @pl.when((step >= 1) & (step <= chunks))
        def _():
            subtract(step - 1)

        @pl.when(step >= 2)
        def _():
            reflect(step - 2)

        return 0

    lax.fori_loop(0, chunks + 2, finish, 0)

    def sent(c, _):
        for tick in range(TICKS - 1):
            @pl.when(i < pieces - 1)
            def _():
                east(tick, c).wait_send()

            @pl.when(j < rows_by - 1)
            def _():
                north(tick, c).wait_send()

        for n in range(count):
            @pl.when(has_relay_to)
            def _():
                relay(c, n).wait_send()

            difference(c, n).wait_send()

        @pl.when(j < rows_by - 1)
        def _():
            final_north(c).wait_send()

        @pl.when(j > 0)
        def _():
            final_south(c).wait_send()

        return 0

    lax.fori_loop(0, chunks, sent, 0)

    if fused:
        for k in range(1, pieces):
            peer = lax.rem(i + k, pieces)
            for part in range(spans):
                cols = pl.ds(part * span, span)
                remote(
                    spec.at[0, 0, :, cols], regroup.at[peer, :, cols], s_send.at[0, 0, part],
                    s_recv.at[peer, part], {"bx": peer},
                ).wait_recv()
        out_ref[...] = regroup[...]
        for c in range(chunks):
            for o in range(per):
                @pl.when(owner(c, o) != i)
                def _():
                    for part in range(spans):
                        regrouped(c, o, part).wait_send()


def shards(source, start_tick, op_x, op_y):
    pieces, rows_by = lax.axis_size("bx"), lax.axis_size("by")
    _, _, _, shots, width = source.shape
    owned = shots // pieces
    fused = owned % 16 == 0 and pieces % CHUNKS == 0
    per, group = (pieces // CHUNKS, owned) if fused else (1, shots // CHUNKS)
    rows = 2 * per * group
    side = 2 * pieces * owned

    cos_line, sin_line = dft_tables(width)
    tables = jnp.asarray(np.concatenate([cos_line, -sin_line]))

    out_shape = (
        jax.ShapeDtypeStruct((pieces, 2 * owned, width), BF16) if fused else jax.ShapeDtypeStruct((2, shots, width), BF16)
    )
    ticked = pltpu.VMEM((TICKS, CHUNKS, rows, width), BF16)
    single = pltpu.VMEM((CHUNKS, rows, width), BF16)
    operator = pltpu.VMEM((2 * width, width), BF16)
    ticked_sem = pltpu.SemaphoreType.DMA((TICKS - 1, CHUNKS))
    tiles = pl.cdiv(width, 256)
    spans = 2 if tiles % 2 == 0 else 1
    tiled_sem = pltpu.SemaphoreType.DMA((CHUNKS, tiles))
    single_sem = pltpu.SemaphoreType.DMA((CHUNKS,))
    result = pl.pallas_call(
        functools.partial(kernel, (pieces, rows_by, per, group, fused, spans)),
        out_shape=out_shape,
        in_specs=[pl.BlockSpec(memory_space=pltpu.SMEM)] + [pl.BlockSpec(memory_space=pl.ANY)] * 4,
        out_specs=pl.BlockSpec(memory_space=pltpu.VMEM),
        scratch_shapes=[
            pltpu.VMEM((2, shots, width), BF16),
            operator, operator,
            pltpu.VMEM(tables.shape, BF16),
            pltpu.VMEM((rows, 2 * width), BF16),
            ticked, ticked, ticked, ticked,
            single, single, single, single, single,
            pltpu.VMEM((CHUNKS, per, 2 * group, width), BF16),
            pltpu.VMEM((pieces, 2 * group, width) if fused else (1, 16, 128), BF16),
            pltpu.SemaphoreType.DMA((2 + 2 * tiles,)),
            ticked_sem, ticked_sem, ticked_sem, ticked_sem,
            tiled_sem, tiled_sem, tiled_sem, tiled_sem,
            single_sem, single_sem, single_sem, single_sem,
            pltpu.SemaphoreType.DMA((CHUNKS, per, spans)),
            pltpu.SemaphoreType.DMA((pieces, spans)),
        ],
        compiler_params=pltpu.CompilerParams(
            collective_id=0, has_side_effects=True, vmem_limit_bytes=60 * 1024 * 1024
        ),
        cost_estimate=pl.CostEstimate(
            flops=2 * rows * CHUNKS * 2 * width * width * 10, bytes_accessed=16 * width * width, transcendentals=0
        ),
    )(
        start_tick,
        source[0, 0],
        op_x.reshape(2 * width, width),
        op_y.reshape(2 * width, width),
        tables,
    )
    if fused:
        grid = jnp.asarray(grid_matrix(pieces, owned))
        gain = jnp.asarray(np.tile(grid_gain(pieces), 2 * owned))
        upgoing = jnp.dot(grid, result.reshape(side, width), preferred_element_type=F32) * gain[:, None]
        return upgoing.reshape(1, owned, 2, pieces, width)
    arranged = result.reshape(2, pieces, owned, 1, width)
    spectrum = lax.all_to_all(arranged, "bx", split_axis=1, concat_axis=3, tiled=True)
    received = spectrum.reshape(2, owned, pieces, width)
    cos_grid, sin_grid = (jnp.asarray(t) for t in dft_tables(pieces))

    def over_grid(values, table):
        return jnp.einsum("sik,iq->sqk", values, table, preferred_element_type=F32)

    out_real = over_grid(received[0], cos_grid) + over_grid(received[1], sin_grid)
    out_imag = over_grid(received[1], cos_grid) - over_grid(received[0], sin_grid)
    upgoing = jnp.stack([out_real, out_imag], axis=1) * grid_gain(pieces)[None, None, :, None]
    return upgoing[None]


def solution(mesh):
    placed = (
        P("bx", "by", None, None, None),
        P("bx", "by"),
        P("bx", "by", None, None, None),
        P("bx", "by", None, None, None),
    )
    return jax.shard_map(
        shards,
        mesh=mesh,
        in_specs=placed,
        out_specs=P("by", "bx", None, None, None),
        check_vma=False,
    )
```

```python
import functools
import math

import jax
import jax.numpy as jnp
import ml_dtypes
import numpy as np
from jax import lax
from jax.experimental import pallas as pl
from jax.experimental.pallas import tpu as pltpu
from jax.sharding import PartitionSpec as P

TICKS = 4
CHUNKS = 2
MESH = pl.DeviceIdType.MESH
BF16 = jnp.bfloat16
F32 = jnp.float32


def dft_tables(length):
    indices = np.arange(length, dtype=np.int64)
    angles = (indices[:, None] * indices[None, :] % length) * (2.0 * math.pi / length)
    return np.cos(angles).astype(ml_dtypes.bfloat16), np.sin(angles).astype(ml_dtypes.bfloat16)


def grid_gain(pieces):
    wave = np.arange(pieces)
    signed = np.where(wave < pieces // 2, wave, wave - pieces).astype(np.float64)
    return (0.5 * (1.0 + signed / np.sqrt(signed * signed + 1.0))).astype(np.float32)


def grid_matrix(pieces, owned):
    cos_grid, sin_grid = (t.astype(np.float32) for t in dft_tables(pieces))
    parts = np.zeros((2, pieces, pieces, 2), np.float32)
    parts[0, :, :, 0] = cos_grid.T
    parts[0, :, :, 1] = sin_grid.T
    parts[1, :, :, 0] = -sin_grid.T
    parts[1, :, :, 1] = cos_grid.T
    full = np.einsum("cqir,st->scqirt", parts, np.eye(owned, dtype=np.float32))
    side = 2 * pieces * owned
    return full.reshape(side, side).astype(ml_dtypes.bfloat16)


def kernel(
    plan,
    first_ref, source_hbm, opx_hbm, opy_hbm, tables_hbm,
    out_ref,
    source_ref, opx, opy, tables, left, e_out, n_out, e_in, n_in, relay_in, d_out, d_in, nf_in, nb_in, spec, regroup,
    load_sem, e_send, e_recv, n_send, n_recv, r_send, r_recv, d_send, d_recv,
    nf_send, nf_recv, nb_send, nb_recv, s_send, s_recv,
):
    pieces, rows_by, per, group, fused, spans = plan
    chunks = CHUNKS
    half = per * group
    width = source_hbm.shape[2]
    tile = min(256, width)
    i, j = lax.axis_index("bx"), lax.axis_index("by")
    odd = lax.rem(i, 2)
    partner = i + 1 - 2 * odd
    relay_to = i - 2 + 4 * odd
    relay_from = i + 2 - 4 * odd
    has_relay_to = (relay_to >= 0) & (relay_to < pieces)
    has_relay_from = (relay_from >= 0) & (relay_from < pieces)

    starts = range(0, width, tile)

    def load(src, dst, k):
        return pltpu.make_async_copy(src, dst, load_sem.at[k])

    def by_tiles(src, dst, k):
        return [
            load(src.at[:, start : start + tile], dst.at[:, start : start + tile], k + n)
            for n, start in enumerate(starts)
        ]

    count = len(starts)
    span = width // spans
    source_load = load(source_hbm, source_ref, 0)
    opx_loads = by_tiles(opx_hbm, opx, 1)
    opy_loads = by_tiles(opy_hbm, opy, 1 + count)
    tables_load = load(tables_hbm, tables, 1 + 2 * count)
    for copy in [source_load, *opx_loads, *opy_loads]:
        copy.start()

    barrier = pltpu.get_barrier_semaphore()
    for k in range(1, pieces):
        pl.semaphore_signal(
            barrier, inc=1, device_id={"bx": lax.rem(i + k, pieces)}, device_id_type=MESH
        )

    @pl.when(j > 0)
    def _():
        pl.semaphore_signal(barrier, inc=1, device_id={"by": j - 1}, device_id_type=MESH)

    @pl.when(j < rows_by - 1)
    def _():
        pl.semaphore_signal(barrier, inc=1, device_id={"by": j + 1}, device_id_type=MESH)

    def clear(ref, tick, c):
        ref[tick, c] = jnp.zeros(ref.shape[2:], ref.dtype)

    def clear_all(c, _):
        clear(e_in, 0, c)
        clear(n_in, 0, c)

        @pl.when(i == 0)
        def _():
            for tick in range(1, TICKS):
                clear(e_in, tick, c)

        @pl.when(j == 0)
        def _():
            for tick in range(1, TICKS):
                clear(n_in, tick, c)
            nf_in[c] = jnp.zeros(nf_in.shape[1:], BF16)

        @pl.when(j == rows_by - 1)
        def _():
            nb_in[c] = jnp.zeros(nb_in.shape[1:], BF16)

        @pl.when(jnp.logical_not(has_relay_from))
        def _():
            relay_in[c] = jnp.zeros(relay_in.shape[1:], BF16)

        return 0

    lax.fori_loop(0, chunks, clear_all, 0)

    peers = pieces - 1 + (j > 0).astype(jnp.int32) + (j < rows_by - 1).astype(jnp.int32)

    def remote(src, dst, send, recv, where):
        return pltpu.make_async_remote_copy(
            src_ref=src, dst_ref=dst, send_sem=send, recv_sem=recv, device_id=where, device_id_type=MESH
        )

    def east(tick, c):
        return remote(
            e_out.at[tick, c], e_in.at[tick + 1, c], e_send.at[tick, c], e_recv.at[tick, c], {"bx": i + 1}
        )

    def north(tick, c):
        return remote(
            n_out.at[tick, c], n_in.at[tick + 1, c], n_send.at[tick, c], n_recv.at[tick, c], {"by": j + 1}
        )

    def relay(c, n):
        cols = pl.ds(starts[n], tile)
        return remote(
            e_out.at[TICKS - 1, c, :, cols], relay_in.at[c, :, cols], r_send.at[c, n], r_recv.at[c, n],
            {"bx": relay_to},
        )

    def difference(c, n):
        cols = pl.ds(starts[n], tile)
        return remote(
            d_out.at[c, :, cols], d_in.at[c, :, cols], d_send.at[c, n], d_recv.at[c, n], {"bx": partner}
        )

    def final_north(c):
        return remote(n_out.at[TICKS - 1, c], nf_in.at[c], nf_send.at[c], nf_recv.at[c], {"by": j + 1})

    def final_south(c):
        return remote(n_out.at[TICKS - 1, c], nb_in.at[c], nb_send.at[c], nb_recv.at[c], {"by": j - 1})

    def owner(c, o):
        if o % 2 == 1 and chunks % 2 == 0:
            return c + 1 - 2 * lax.rem(c, 2) + chunks * o
        return c + chunks * o

    def regrouped(c, o, part):
        cols = pl.ds(part * span, span)
        return remote(
            spec.at[c, o, :, cols], regroup.at[i, :, cols], s_send.at[c, o, part], s_recv.at[i, part],
            {"bx": owner(c, o)},
        )

    def shot_rows(c, o):
        return pl.ds(pl.multiple_of(owner(c, o) * group, group), group)

    def place(part, at, size, value):
        if part == 0:
            left[at : at + size, :width] = value
            left[half + at : half + at + size, width:] = value
        else:
            left[at : at + size, width:] = -value
            left[half + at : half + at + size, :width] = value

    def product(matrix, put, loads=None, then=None):
        for n, start in enumerate(starts):
            cols = slice(start, start + tile)
            if loads is not None:
                loads[n].wait()
            got = jnp.dot(left[...], matrix[:, cols], preferred_element_type=F32)
            put(cols, got.astype(BF16))
            if then is not None:
                then(n)

    def incident(tick, c):
        active = (first_ref[0, 0] <= tick).astype(F32)
        for part in range(2):
            for o in range(per):
                at = o * group
                rows = slice(part * half + at, part * half + at + group)
                value = (
                    e_in[tick, c, rows, :].astype(F32)
                    + n_in[tick, c, rows, :].astype(F32)
                    + active * source_ref[part, shot_rows(c, o), :].astype(F32)
                )
                place(part, at, group, value.astype(BF16))

    def arrive(tick, c):
        @pl.when(i > 0)
        def _():
            east(tick - 1, c).wait_recv()

        @pl.when(j > 0)
        def _():
            north(tick - 1, c).wait_recv()

    def sweep(step, _, first=False):
        tick, c = (0, 0) if first else (step // chunks, lax.rem(step, chunks))

        if not first:
            @pl.when(tick > 0)
            def _():
                arrive(tick, c)

        incident(tick, c)

        def put_east(cols, value):
            e_out[tick, c, :, cols] = value

        product(opx, put_east, opx_loads if first else None)
        if first:
            pl.semaphore_wait(barrier, peers)

        @pl.when(i < pieces - 1)
        def _():
            east(tick, c).start()

        def put_north(cols, value):
            n_out[tick, c, :, cols] = value

        product(opy, put_north, opy_loads if first else None)

        @pl.when(j < rows_by - 1)
        def _():
            north(tick, c).start()

        return 0

    source_load.wait()
    sweep(0, 0, first=True)
    tables_load.start()
    lax.fori_loop(1, (TICKS - 1) * chunks, sweep, 0)
    tables_load.wait()
    last = TICKS - 1

    def last_east(c):
        arrive(last, c)
        incident(last, c)

        def put_east(cols, value):
            e_out[last, c, :, cols] = value

        def send_east(n):
            @pl.when(has_relay_to)
            def _():
                relay(c, n).start()

        product(opx, put_east, then=send_east)

    def last_north(c):
        def put_north(cols, value):
            n_out[last, c, :, cols] = value

        product(opy, put_north)

        @pl.when(j < rows_by - 1)
        def _():
            final_north(c).start()

        @pl.when(j > 0)
        def _():
            final_south(c).start()

    def subtract(c):
        sign = (2 * odd - 1).astype(F32)
        for n, start in enumerate(starts):
            @pl.when(has_relay_from)
            def _():
                relay(c, n).wait_recv()

            cols = slice(start, start + tile)
            value = relay_in[c, :, cols].astype(F32) - e_out[last, c, :, cols].astype(F32)
            d_out[c, :, cols] = (sign * value).astype(BF16)
            difference(c, n).start()

    def reflect(c):
        for n in range(count):
            difference(c, n).wait_recv()

        @pl.when(j > 0)
        def _():
            final_north(c).wait_recv()

        @pl.when(j < rows_by - 1)
        def _():
            final_south(c).wait_recv()

        for part in range(2):
            rows = slice(part * half, (part + 1) * half)
            value = (
                d_in[c, rows, :].astype(F32) + nf_in[c, rows, :].astype(F32) - nb_in[c, rows, :].astype(F32)
            )
            place(part, 0, half, value.astype(BF16))

        def put_reflected(cols, value):
            d_out_free[:, cols] = value

        d_out_free = e_in.at[0, c]
        product(opx, put_reflected)
        for part in range(2):
            place(part, 0, half, d_out_free[part * half : (part + 1) * half, :])

        def put_spectrum(cols, value):
            for part in range(2):
                for o in range(per):
                    at = part * half + o * group
                    if fused:
                        spec[c, o, part * group : (part + 1) * group, cols] = value[at : at + group]
                    else:
                        out_ref[part, shot_rows(c, o), cols] = value[at : at + group]

        def send_spectrum(n):
            if not fused or (n + 1) * spans % count:
                return
            part = (n + 1) * spans // count - 1
            cols = slice(part * span, (part + 1) * span)
            for o in range(per):
                @pl.when(owner(c, o) == i)
                def _():
                    regroup[i, :, cols] = spec[c, o, :, cols]

                @pl.when(owner(c, o) != i)
                def _():
                    regrouped(c, o, part).start()

        product(tables, put_spectrum, then=send_spectrum)

    def finish(step, _):
        @pl.when(step < chunks)
        def _():
            last_east(step)

        @pl.when((step >= 1) & (step <= chunks))
        def _():
            subtract(step - 1)

        @pl.when(step < chunks)
        def _():
            last_north(step)

        @pl.when(step >= 2)
        def _():
            reflect(step - 2)

        return 0

    lax.fori_loop(0, chunks + 2, finish, 0)

    def sent(c, _):
        for tick in range(TICKS - 1):
            @pl.when(i < pieces - 1)
            def _():
                east(tick, c).wait_send()

            @pl.when(j < rows_by - 1)
            def _():
                north(tick, c).wait_send()

        for n in range(count):
            @pl.when(has_relay_to)
            def _():
                relay(c, n).wait_send()

            difference(c, n).wait_send()

        @pl.when(j < rows_by - 1)
        def _():
            final_north(c).wait_send()

        @pl.when(j > 0)
        def _():
            final_south(c).wait_send()

        return 0

    lax.fori_loop(0, chunks, sent, 0)

    if fused:
        for k in range(1, pieces):
            peer = lax.rem(i + k, pieces)
            for part in range(spans):
                cols = pl.ds(part * span, span)
                remote(
                    spec.at[0, 0, :, cols], regroup.at[peer, :, cols], s_send.at[0, 0, part],
                    s_recv.at[peer, part], {"bx": peer},
                ).wait_recv()
        out_ref[...] = regroup[...]
        for c in range(chunks):
            for o in range(per):
                @pl.when(owner(c, o) != i)
                def _():
                    for part in range(spans):
                        regrouped(c, o, part).wait_send()


def shards(source, start_tick, op_x, op_y):
    pieces, rows_by = lax.axis_size("bx"), lax.axis_size("by")
    _, _, _, shots, width = source.shape
    owned = shots // pieces
    fused = owned % 16 == 0 and pieces % CHUNKS == 0
    per, group = (pieces // CHUNKS, owned) if fused else (1, shots // CHUNKS)
    rows = 2 * per * group
    side = 2 * pieces * owned

    cos_line, sin_line = dft_tables(width)
    tables = jnp.asarray(np.concatenate([cos_line, -sin_line]))

    out_shape = (
        jax.ShapeDtypeStruct((pieces, 2 * owned, width), BF16) if fused else jax.ShapeDtypeStruct((2, shots, width), BF16)
    )
    ticked = pltpu.VMEM((TICKS, CHUNKS, rows, width), BF16)
    single = pltpu.VMEM((CHUNKS, rows, width), BF16)
    operator = pltpu.VMEM((2 * width, width), BF16)
    ticked_sem = pltpu.SemaphoreType.DMA((TICKS - 1, CHUNKS))
    tiles = pl.cdiv(width, 256)
    spans = 2 if tiles % 2 == 0 else 1
    tiled_sem = pltpu.SemaphoreType.DMA((CHUNKS, tiles))
    single_sem = pltpu.SemaphoreType.DMA((CHUNKS,))
    result = pl.pallas_call(
        functools.partial(kernel, (pieces, rows_by, per, group, fused, spans)),
        out_shape=out_shape,
        in_specs=[pl.BlockSpec(memory_space=pltpu.SMEM)] + [pl.BlockSpec(memory_space=pl.ANY)] * 4,
        out_specs=pl.BlockSpec(memory_space=pltpu.VMEM),
        scratch_shapes=[
            pltpu.VMEM((2, shots, width), BF16),
            operator, operator,
            pltpu.VMEM(tables.shape, BF16),
            pltpu.VMEM((rows, 2 * width), BF16),
            ticked, ticked, ticked, ticked,
            single, single, single, single, single,
            pltpu.VMEM((CHUNKS, per, 2 * group, width), BF16),
            pltpu.VMEM((pieces, 2 * group, width) if fused else (1, 16, 128), BF16),
            pltpu.SemaphoreType.DMA((2 + 2 * tiles,)),
            ticked_sem, ticked_sem, ticked_sem, ticked_sem,
            tiled_sem, tiled_sem, tiled_sem, tiled_sem,
            single_sem, single_sem, single_sem, single_sem,
            pltpu.SemaphoreType.DMA((CHUNKS, per, spans)),
            pltpu.SemaphoreType.DMA((pieces, spans)),
        ],
        compiler_params=pltpu.CompilerParams(
            collective_id=0, has_side_effects=True, vmem_limit_bytes=60 * 1024 * 1024
        ),
        cost_estimate=pl.CostEstimate(
            flops=2 * rows * CHUNKS * 2 * width * width * 10, bytes_accessed=16 * width * width, transcendentals=0
        ),
    )(
        start_tick,
        source[0, 0],
        op_x.reshape(2 * width, width),
        op_y.reshape(2 * width, width),
        tables,
    )
    if fused:
        grid = jnp.asarray(grid_matrix(pieces, owned))
        gain = jnp.asarray(np.tile(grid_gain(pieces), 2 * owned))
        upgoing = jnp.dot(grid, result.reshape(side, width), preferred_element_type=F32) * gain[:, None]
        return upgoing.reshape(1, owned, 2, pieces, width)
    arranged = result.reshape(2, pieces, owned, 1, width)
    spectrum = lax.all_to_all(arranged, "bx", split_axis=1, concat_axis=3, tiled=True)
    received = spectrum.reshape(2, owned, pieces, width)
    cos_grid, sin_grid = (jnp.asarray(t) for t in dft_tables(pieces))

    def over_grid(values, table):
        return jnp.einsum("sik,iq->sqk", values, table, preferred_element_type=F32)

    out_real = over_grid(received[0], cos_grid) + over_grid(received[1], sin_grid)
    out_imag = over_grid(received[1], cos_grid) - over_grid(received[0], sin_grid)
    upgoing = jnp.stack([out_real, out_imag], axis=1) * grid_gain(pieces)[None, None, :, None]
    return upgoing[None]


def solution(mesh):
    placed = (
        P("bx", "by", None, None, None),
        P("bx", "by"),
        P("bx", "by", None, None, None),
        P("bx", "by", None, None, None),
    )
    return jax.shard_map(
        shards,
        mesh=mesh,
        in_specs=placed,
        out_specs=P("by", "bx", None, None, None),
        check_vma=False,
    )
```

```python
import functools
import math

import jax
import jax.numpy as jnp
import ml_dtypes
import numpy as np
from jax import lax
from jax.experimental import pallas as pl
from jax.experimental.pallas import tpu as pltpu
from jax.sharding import PartitionSpec as P

TICKS = 4
CHUNKS = 2
MESH = pl.DeviceIdType.MESH
BF16 = jnp.bfloat16
F32 = jnp.float32


def dft_tables(length):
    indices = np.arange(length, dtype=np.int64)
    angles = (indices[:, None] * indices[None, :] % length) * (2.0 * math.pi / length)
    return np.cos(angles).astype(ml_dtypes.bfloat16), np.sin(angles).astype(ml_dtypes.bfloat16)


def grid_gain(pieces):
    wave = np.arange(pieces)
    signed = np.where(wave < pieces // 2, wave, wave - pieces).astype(np.float64)
    return (0.5 * (1.0 + signed / np.sqrt(signed * signed + 1.0))).astype(np.float32)


def grid_matrix(pieces, owned):
    cos_grid, sin_grid = (t.astype(np.float32) for t in dft_tables(pieces))
    parts = np.zeros((2, pieces, pieces, 2), np.float32)
    parts[0, :, :, 0] = cos_grid.T
    parts[0, :, :, 1] = sin_grid.T
    parts[1, :, :, 0] = -sin_grid.T
    parts[1, :, :, 1] = cos_grid.T
    full = np.einsum("cqir,st->scqirt", parts, np.eye(owned, dtype=np.float32))
    side = 2 * pieces * owned
    return full.reshape(side, side).astype(ml_dtypes.bfloat16)


def kernel(
    plan,
    first_ref, source_hbm, opx_hbm, opy_hbm, tables_hbm,
    out_ref,
    source_ref, opx, opy, tables, left, e_out, n_out, e_in, n_in, relay_in, d_out, d_in, nf_in, nb_in, spec, regroup,
    load_sem, e_send, e_recv, n_send, n_recv, r_send, r_recv, d_send, d_recv,
    nf_send, nf_recv, nb_send, nb_recv, s_send, s_recv,
):
    pieces, rows_by, per, group, fused, spans = plan
    chunks = CHUNKS
    half = per * group
    width = source_hbm.shape[2]
    tile = min(256, width)
    i, j = lax.axis_index("bx"), lax.axis_index("by")
    odd = lax.rem(i, 2)
    partner = i + 1 - 2 * odd
    relay_to = i - 2 + 4 * odd
    relay_from = i + 2 - 4 * odd
    has_relay_to = (relay_to >= 0) & (relay_to < pieces)
    has_relay_from = (relay_from >= 0) & (relay_from < pieces)

    starts = range(0, width, tile)

    def load(src, dst, k):
        return pltpu.make_async_copy(src, dst, load_sem.at[k])

    def by_tiles(src, dst, k):
        return [
            load(src.at[:, start : start + tile], dst.at[:, start : start + tile], k + n)
            for n, start in enumerate(starts)
        ]

    count = len(starts)
    span = width // spans
    source_load = load(source_hbm, source_ref, 0)
    opx_loads = by_tiles(opx_hbm, opx, 1)
    opy_loads = by_tiles(opy_hbm, opy, 1 + count)
    tables_load = load(tables_hbm, tables, 1 + 2 * count)
    for copy in [source_load, *opx_loads, *opy_loads]:
        copy.start()

    barrier = pltpu.get_barrier_semaphore()
    for k in range(1, pieces):
        pl.semaphore_signal(
            barrier, inc=1, device_id={"bx": lax.rem(i + k, pieces)}, device_id_type=MESH
        )

    @pl.when(j > 0)
    def _():
        pl.semaphore_signal(barrier, inc=1, device_id={"by": j - 1}, device_id_type=MESH)

    @pl.when(j < rows_by - 1)
    def _():
        pl.semaphore_signal(barrier, inc=1, device_id={"by": j + 1}, device_id_type=MESH)

    def clear(ref, tick, c):
        ref[tick, c] = jnp.zeros(ref.shape[2:], ref.dtype)

    def clear_all(c, _):
        clear(e_in, 0, c)
        clear(n_in, 0, c)

        @pl.when(i == 0)
        def _():
            for tick in range(1, TICKS):
                clear(e_in, tick, c)

        @pl.when(j == 0)
        def _():
            for tick in range(1, TICKS):
                clear(n_in, tick, c)
            nf_in[c] = jnp.zeros(nf_in.shape[1:], BF16)

        @pl.when(j == rows_by - 1)
        def _():
            nb_in[c] = jnp.zeros(nb_in.shape[1:], BF16)

        @pl.when(jnp.logical_not(has_relay_from))
        def _():
            relay_in[c] = jnp.zeros(relay_in.shape[1:], BF16)

        return 0

    lax.fori_loop(0, chunks, clear_all, 0)

    peers = pieces - 1 + (j > 0).astype(jnp.int32) + (j < rows_by - 1).astype(jnp.int32)

    def remote(src, dst, send, recv, where):
        return pltpu.make_async_remote_copy(
            src_ref=src, dst_ref=dst, send_sem=send, recv_sem=recv, device_id=where, device_id_type=MESH
        )

    def east(tick, c, part):
        cols = pl.ds(part * span, span)
        return remote(
            e_out.at[tick, c, :, cols], e_in.at[tick + 1, c, :, cols], e_send.at[tick, c, part],
            e_recv.at[tick, c, part], {"bx": i + 1},
        )

    def north(tick, c):
        return remote(
            n_out.at[tick, c], n_in.at[tick + 1, c], n_send.at[tick, c], n_recv.at[tick, c], {"by": j + 1}
        )

    def relay(c, n):
        cols = pl.ds(starts[n], tile)
        return remote(
            e_out.at[TICKS - 1, c, :, cols], relay_in.at[c, :, cols], r_send.at[c, n], r_recv.at[c, n],
            {"bx": relay_to},
        )

    def difference(c, n):
        cols = pl.ds(starts[n], tile)
        return remote(
            d_out.at[c, :, cols], d_in.at[c, :, cols], d_send.at[c, n], d_recv.at[c, n], {"bx": partner}
        )

    def final_north(c):
        return remote(n_out.at[TICKS - 1, c], nf_in.at[c], nf_send.at[c], nf_recv.at[c], {"by": j + 1})

    def final_south(c):
        return remote(n_out.at[TICKS - 1, c], nb_in.at[c], nb_send.at[c], nb_recv.at[c], {"by": j - 1})

    def owner(c, o):
        if o % 2 == 1 and chunks % 2 == 0:
            return c + 1 - 2 * lax.rem(c, 2) + chunks * o
        return c + chunks * o

    def regrouped(c, o, part):
        cols = pl.ds(part * span, span)
        return remote(
            spec.at[c, o, :, cols], regroup.at[i, :, cols], s_send.at[c, o, part], s_recv.at[i, part],
            {"bx": owner(c, o)},
        )

    def shot_rows(c, o):
        return pl.ds(pl.multiple_of(owner(c, o) * group, group), group)

    def place(part, at, size, value):
        if part == 0:
            left[at : at + size, :width] = value
            left[half + at : half + at + size, width:] = value
        else:
            left[at : at + size, width:] = -value
            left[half + at : half + at + size, :width] = value

    def product(matrix, put, loads=None, then=None):
        for n, start in enumerate(starts):
            cols = slice(start, start + tile)
            if loads is not None:
                loads[n].wait()
            got = jnp.dot(left[...], matrix[:, cols], preferred_element_type=F32)
            put(cols, got.astype(BF16))
            if then is not None:
                then(n)

    def incident(tick, c):
        active = (first_ref[0, 0] <= tick).astype(F32)
        for part in range(2):
            for o in range(per):
                at = o * group
                rows = slice(part * half + at, part * half + at + group)
                value = (
                    e_in[tick, c, rows, :].astype(F32)
                    + n_in[tick, c, rows, :].astype(F32)
                    + active * source_ref[part, shot_rows(c, o), :].astype(F32)
                )
                place(part, at, group, value.astype(BF16))

    def arrive(tick, c):
        @pl.when(i > 0)
        def _():
            for part in range(spans):
                east(tick - 1, c, part).wait_recv()

        @pl.when(j > 0)
        def _():
            north(tick - 1, c).wait_recv()

    def sweep(step, _, first=False):
        tick, c = (0, 0) if first else (step // chunks, lax.rem(step, chunks))

        if not first:
            @pl.when(tick > 0)
            def _():
                arrive(tick, c)

        incident(tick, c)

        def put_east(cols, value):
            e_out[tick, c, :, cols] = value

        def send_east(n):
            if (n + 1) * spans % count:
                return
            part = (n + 1) * spans // count - 1
            if first and part == 0:
                pl.semaphore_wait(barrier, peers)

            @pl.when(i < pieces - 1)
            def _():
                east(tick, c, part).start()

        product(opx, put_east, opx_loads if first else None, send_east)

        def put_north(cols, value):
            n_out[tick, c, :, cols] = value

        product(opy, put_north, opy_loads if first else None)

        @pl.when(j < rows_by - 1)
        def _():
            north(tick, c).start()

        return 0

    source_load.wait()
    sweep(0, 0, first=True)
    tables_load.start()
    lax.fori_loop(1, (TICKS - 1) * chunks, sweep, 0)
    tables_load.wait()
    last = TICKS - 1

    def last_east(c):
        arrive(last, c)
        incident(last, c)

        def put_east(cols, value):
            e_out[last, c, :, cols] = value

        def send_east(n):
            @pl.when(has_relay_to)
            def _():
                relay(c, n).start()

        product(opx, put_east, then=send_east)

    def last_north(c):
        def put_north(cols, value):
            n_out[last, c, :, cols] = value

        product(opy, put_north)

        @pl.when(j < rows_by - 1)
        def _():
            final_north(c).start()

        @pl.when(j > 0)
        def _():
            final_south(c).start()

    def subtract(c):
        sign = (2 * odd - 1).astype(F32)
        for n, start in enumerate(starts):
            @pl.when(has_relay_from)
            def _():
                relay(c, n).wait_recv()

            cols = slice(start, start + tile)
            value = relay_in[c, :, cols].astype(F32) - e_out[last, c, :, cols].astype(F32)
            d_out[c, :, cols] = (sign * value).astype(BF16)
            difference(c, n).start()

    def reflect(c):
        for n in range(count):
            difference(c, n).wait_recv()

        @pl.when(j > 0)
        def _():
            final_north(c).wait_recv()

        @pl.when(j < rows_by - 1)
        def _():
            final_south(c).wait_recv()

        for part in range(2):
            rows = slice(part * half, (part + 1) * half)
            value = (
                d_in[c, rows, :].astype(F32) + nf_in[c, rows, :].astype(F32) - nb_in[c, rows, :].astype(F32)
            )
            place(part, 0, half, value.astype(BF16))

        def put_reflected(cols, value):
            d_out_free[:, cols] = value

        d_out_free = e_in.at[0, c]
        product(opx, put_reflected)
        for part in range(2):
            place(part, 0, half, d_out_free[part * half : (part + 1) * half, :])

        def put_spectrum(cols, value):
            for part in range(2):
                for o in range(per):
                    at = part * half + o * group
                    if fused:
                        spec[c, o, part * group : (part + 1) * group, cols] = value[at : at + group]
                    else:
                        out_ref[part, shot_rows(c, o), cols] = value[at : at + group]

        def send_spectrum(n):
            if not fused or (n + 1) * spans % count:
                return
            part = (n + 1) * spans // count - 1
            cols = slice(part * span, (part + 1) * span)
            for o in range(per):
                @pl.when(owner(c, o) == i)
                def _():
                    regroup[i, :, cols] = spec[c, o, :, cols]

                @pl.when(owner(c, o) != i)
                def _():
                    regrouped(c, o, part).start()

        product(tables, put_spectrum, then=send_spectrum)

    def finish(step, _):
        @pl.when(step < chunks)
        def _():
            last_east(step)

        @pl.when((step >= 1) & (step <= chunks))
        def _():
            subtract(step - 1)

        @pl.when(step < chunks)
        def _():
            last_north(step)

        @pl.when(step >= 2)
        def _():
            reflect(step - 2)

        return 0

    lax.fori_loop(0, chunks + 2, finish, 0)

    def sent(c, _):
        for tick in range(TICKS - 1):
            @pl.when(i < pieces - 1)
            def _():
                for part in range(spans):
                    east(tick, c, part).wait_send()

            @pl.when(j < rows_by - 1)
            def _():
                north(tick, c).wait_send()

        for n in range(count):
            @pl.when(has_relay_to)
            def _():
                relay(c, n).wait_send()

            difference(c, n).wait_send()

        @pl.when(j < rows_by - 1)
        def _():
            final_north(c).wait_send()

        @pl.when(j > 0)
        def _():
            final_south(c).wait_send()

        return 0

    lax.fori_loop(0, chunks, sent, 0)

    if fused:
        for k in range(1, pieces):
            peer = lax.rem(i + k, pieces)
            for part in range(spans):
                cols = pl.ds(part * span, span)
                remote(
                    spec.at[0, 0, :, cols], regroup.at[peer, :, cols], s_send.at[0, 0, part],
                    s_recv.at[peer, part], {"bx": peer},
                ).wait_recv()
        out_ref[...] = regroup[...]
        for c in range(chunks):
            for o in range(per):
                @pl.when(owner(c, o) != i)
                def _():
                    for part in range(spans):
                        regrouped(c, o, part).wait_send()


def shards(source, start_tick, op_x, op_y):
    pieces, rows_by = lax.axis_size("bx"), lax.axis_size("by")
    _, _, _, shots, width = source.shape
    owned = shots // pieces
    fused = owned % 16 == 0 and pieces % CHUNKS == 0
    per, group = (pieces // CHUNKS, owned) if fused else (1, shots // CHUNKS)
    rows = 2 * per * group
    side = 2 * pieces * owned

    cos_line, sin_line = dft_tables(width)
    tables = jnp.asarray(np.concatenate([cos_line, -sin_line]))

    out_shape = (
        jax.ShapeDtypeStruct((pieces, 2 * owned, width), BF16) if fused else jax.ShapeDtypeStruct((2, shots, width), BF16)
    )
    ticked = pltpu.VMEM((TICKS, CHUNKS, rows, width), BF16)
    single = pltpu.VMEM((CHUNKS, rows, width), BF16)
    operator = pltpu.VMEM((2 * width, width), BF16)
    ticked_sem = pltpu.SemaphoreType.DMA((TICKS - 1, CHUNKS))
    tiles = pl.cdiv(width, 256)
    spans = 2 if tiles % 2 == 0 else 1
    halved_sem = pltpu.SemaphoreType.DMA((TICKS - 1, CHUNKS, spans))
    tiled_sem = pltpu.SemaphoreType.DMA((CHUNKS, tiles))
    single_sem = pltpu.SemaphoreType.DMA((CHUNKS,))
    result = pl.pallas_call(
        functools.partial(kernel, (pieces, rows_by, per, group, fused, spans)),
        out_shape=out_shape,
        in_specs=[pl.BlockSpec(memory_space=pltpu.SMEM)] + [pl.BlockSpec(memory_space=pl.ANY)] * 4,
        out_specs=pl.BlockSpec(memory_space=pltpu.VMEM),
        scratch_shapes=[
            pltpu.VMEM((2, shots, width), BF16),
            operator, operator,
            pltpu.VMEM(tables.shape, BF16),
            pltpu.VMEM((rows, 2 * width), BF16),
            ticked, ticked, ticked, ticked,
            single, single, single, single, single,
            pltpu.VMEM((CHUNKS, per, 2 * group, width), BF16),
            pltpu.VMEM((pieces, 2 * group, width) if fused else (1, 16, 128), BF16),
            pltpu.SemaphoreType.DMA((2 + 2 * tiles,)),
            halved_sem, halved_sem, ticked_sem, ticked_sem,
            tiled_sem, tiled_sem, tiled_sem, tiled_sem,
            single_sem, single_sem, single_sem, single_sem,
            pltpu.SemaphoreType.DMA((CHUNKS, per, spans)),
            pltpu.SemaphoreType.DMA((pieces, spans)),
        ],
        compiler_params=pltpu.CompilerParams(
            collective_id=0, has_side_effects=True, vmem_limit_bytes=60 * 1024 * 1024
        ),
        cost_estimate=pl.CostEstimate(
            flops=2 * rows * CHUNKS * 2 * width * width * 10, bytes_accessed=16 * width * width, transcendentals=0
        ),
    )(
        start_tick,
        source[0, 0],
        op_x.reshape(2 * width, width),
        op_y.reshape(2 * width, width),
        tables,
    )
    if fused:
        grid = jnp.asarray(grid_matrix(pieces, owned))
        gain = jnp.asarray(np.tile(grid_gain(pieces), 2 * owned))
        upgoing = jnp.dot(grid, result.reshape(side, width), preferred_element_type=F32) * gain[:, None]
        return upgoing.reshape(1, owned, 2, pieces, width)
    arranged = result.reshape(2, pieces, owned, 1, width)
    spectrum = lax.all_to_all(arranged, "bx", split_axis=1, concat_axis=3, tiled=True)
    received = spectrum.reshape(2, owned, pieces, width)
    cos_grid, sin_grid = (jnp.asarray(t) for t in dft_tables(pieces))

    def over_grid(values, table):
        return jnp.einsum("sik,iq->sqk", values, table, preferred_element_type=F32)

    out_real = over_grid(received[0], cos_grid) + over_grid(received[1], sin_grid)
    out_imag = over_grid(received[1], cos_grid) - over_grid(received[0], sin_grid)
    upgoing = jnp.stack([out_real, out_imag], axis=1) * grid_gain(pieces)[None, None, :, None]
    return upgoing[None]


def solution(mesh):
    placed = (
        P("bx", "by", None, None, None),
        P("bx", "by"),
        P("bx", "by", None, None, None),
        P("bx", "by", None, None, None),
    )
    return jax.shard_map(
        shards,
        mesh=mesh,
        in_specs=placed,
        out_specs=P("by", "bx", None, None, None),
        check_vma=False,
    )
```
